128 devices in a mesh: ctx: 32 (over z, x, core), head: 4 (over y).
Axes of the slice: x: 4, y: 4, z: 4, core: 2. Of those that a mesh axis runs over, the one named last changes fastest.
Arguments:
- queries: bfloat16 [16384, 7168], P(('ctx', 'head')), may hold values from -6 to 6
- keys_in: bfloat16 [16384, 7168], P(('ctx', 'head')), may hold values from -6 to 6
- values_in: bfloat16 [16384, 7168], P(('ctx', 'head')), may hold values from -6 to 6
- ssm_input: bfloat16 [16384, 7168], P('ctx', 'head'), may hold values from -6 to 6
- step_size: float32 [16384, 112], P('ctx', 'head'), may hold values from 0.5 to 2
- in_proj_b: bfloat16 [16384, 128], P('ctx'), may hold values from -6 to 6
- out_proj_c: bfloat16 [16384, 128], P('ctx'), may hold values from -0.75 to 0.75
- decay_rate: float32 [112], P('head'), may hold values from 0.0001 to 0.05
- skip_gain: float32 [112], P('head'), may hold values from 0.5 to 1.5
- doc_lengths: int32 [64], replicated, may hold values from 1 to 1536, 16384 in all
Outputs:
- attn_out: bfloat16 [16384, 7168], P(('ctx', 'head'))
- ssm_out: bfloat16 [16384, 7168], P('ctx', 'head')
The draws below stay inside these ranges and needn't reach their ends.
Inputs may be any that keep to these rules, and one draw needn't show every extreme that they name: `doc_lengths`: the lengths sum to 16384; the longest is exactly 1536.
All inputs are finite; a program needn't handle non-finite values.
Results may differ from the reference program's by a relative error of at most 0.003.
Values may be sent and summed in bfloat16 or wider, within the bound.
No kernel may reach another device: no remote copies, remote signals or barrier semaphores. Data moves between devices by JAX's collectives and lax.ppermute only.
A program may use at most 256 MiB of HBM per device.

```python
import math
import jax
import jax.numpy as jnp
import numpy as np
from jax import lax

ATT_HEADS = 32
ATT_HD = 224
M_HEADS = 112
M_HD = 64
M_STATE = 64
M_GROUPS = 2
SCAN_LEN = 256
TOK_DEV = 512
D_ATT = 7168
TOKENS = 16384
MOST_DOC = 1536
NUM_DOCS = 64
N_CTX = 32


def aligned_rows(key):
    mark_key, level_key, sign_key = jax.random.split(key, 3)
    order = jnp.arange(TOKENS)
    picked = jnp.logical_and(jax.random.randint(mark_key, (TOKENS,), 0, 64) == 0, order >= 1)
    level = jax.random.randint(level_key, (TOKENS,), 0, 3)
    strength = jnp.where(level == 0, 3.0, jnp.where(level == 1, 4.5, 6.0)).astype(jnp.float32)
    signs = (2 * jax.random.randint(sign_key, (TOKENS, D_ATT), 0, 2) - 1).astype(jnp.float32)
    return (picked, strength, signs)


def draw_queries(key, part):
    picked, strength, signs = aligned_rows(key)
    key = jax.random.fold_in(key, 11)
    background = jax.random.truncated_normal(key, -6.0, 6.0, (TOKENS, D_ATT), jnp.float32)
    planted = jnp.where(picked[:, None], strength[:, None] * signs, background)
    return planted.astype(jnp.bfloat16)


def draw_keys_in(key, part):
    picked, strength, signs = aligned_rows(key)
    key = jax.random.fold_in(key, 12)
    background = jax.random.truncated_normal(key, -6.0, 6.0, (TOKENS, D_ATT), jnp.float32)
    step_down = 0.03125 * max(1, int(15.0 / math.sqrt(ATT_HD)))
    next_picked = jnp.concatenate([picked[1:], jnp.zeros((1,), jnp.bool_)], axis=0)
    next_signs = jnp.concatenate([signs[1:], signs[:1]], axis=0)
    planted = jnp.where(next_picked[:, None], (6.0 - step_down) * next_signs, background)
    planted = jnp.where(picked[:, None], 6.0 * signs, planted)
    return planted.astype(jnp.bfloat16)


def block_scale(own_key, dims, cuts, least, top_value):
    def one(position, parts):
        heights = jax.random.uniform(jax.random.fold_in(jax.random.fold_in(own_key, 6), position), (parts,), jnp.float32, least / len(cuts), top_value / len(cuts))
        return jnp.repeat(jnp.exp(heights), dims[position] // parts).reshape((-1,) + (1,) * (len(dims) - position - 1))

    factor_of = one(*cuts[0])
    for cut in cuts[1:]:
        factor_of = factor_of * one(*cut)
    return factor_of


def split_up(amount, total, reach, lean):
    weights = [(1 << 20) // math.isqrt(rank ** lean) + 1 for rank in range(2, amount + 1)]
    spare, counts = total - reach - (amount - 1), [1] * (amount - 1)
    while spare > 0:
        free = [i for i in range(amount - 1) if counts[i] < reach]
        mass, budget = sum([weights[i] for i in free]), spare
        for i in free:
            extra = min(reach - counts[i], max(1, budget * weights[i] // mass), spare)
            counts[i] = counts[i] + extra
            spare = spare - extra
    return np.array([reach] + counts)


def uneven_parts(own_key, amount, total, bound, skew):
    if amount == 2:
        one = jax.random.randint(own_key, (), max(1, total - bound), min(bound, total - 1) + 1)
        return jnp.stack([one, total - one])
    tallies = jnp.asarray(split_up(amount, total, bound, skew), jnp.int32)
    twos = (amount - 1) // 2
    giver, receiver = tallies[1:1 + 2 * twos:2], tallies[2:2 + 2 * twos:2]
    margin = jnp.minimum(giver - 1, bound - receiver)
    passed = jax.random.randint(jax.random.fold_in(own_key, 1), (twos,), 0, 1 << 20) % (margin + 1)
    tallies = tallies.at[1:1 + 2 * twos:2].set(giver - passed).at[2:2 + 2 * twos:2].set(receiver + passed)
    return tallies[jax.random.permutation(jax.random.fold_in(own_key, 2), amount)]


def noise(rng, extent, spread, bound, shards=(), held_as=jnp.bfloat16):
    entries = jax.random.normal(rng, extent, jnp.float32) * spread
    if len(shards) > 0:
        entries = block_scale(rng, extent, shards, -0.22, 0.18) * entries
    return jnp.clip(entries, min=-bound, max=bound).astype(held_as)


def setup_inputs(seed: int = 0) -> dict:
    seeds = jax.random.split(jax.random.key(seed), 11)
    return {
        "queries": draw_queries(jax.random.fold_in(seeds[10], 71), 0),
        "keys_in": draw_keys_in(jax.random.fold_in(seeds[10], 71), 0),
        "values_in": noise(seeds[2], (TOKENS, D_ATT), 1.0, 6.0, ((0, 128),)),
        "ssm_input": noise(seeds[3], (TOKENS, M_HEADS * M_HD), 1.0, 6.0, ((0, 32), (1, 4))),
        "step_size": jnp.clip(jnp.exp(math.log(2.0) - 1.3862944 * jax.random.uniform(seeds[4], (TOKENS, M_HEADS), jnp.float32) ** block_scale(seeds[4], (TOKENS, M_HEADS), ((0, 32), (1, 4)), -0.2, 0.2)), 0.5, 2.0),
        "in_proj_b": noise(seeds[5], (TOKENS, M_GROUPS * M_STATE), 1.0, 6.0, ((0, 32),)),
        "out_proj_c": noise(seeds[6], (TOKENS, M_GROUPS * M_STATE), M_STATE ** -0.5, 0.75, ((0, 32),)),
        "decay_rate": jnp.clip(jnp.exp(math.log(0.05) - 6.214608 * jax.random.uniform(seeds[7], (M_HEADS,), jnp.float32) ** block_scale(seeds[7], (M_HEADS,), ((0, 4),), -0.2, 0.2)), 0.0001, 0.05),
        "skip_gain": jnp.clip(0.5 + 1.0 * jax.random.uniform(seeds[8], (M_HEADS,), jnp.float32) ** block_scale(seeds[8], (M_HEADS,), ((0, 4),), -0.2, 0.2), 0.5, 1.5),
        "doc_lengths": uneven_parts(seeds[9], NUM_DOCS, TOKENS, MOST_DOC, 2).astype(jnp.int32),
    }


def doc_of(positions, doc_lengths):
    ends = jnp.cumsum(doc_lengths).astype(jnp.int32)
    count = jnp.sum((ends[None, :] <= positions[:, None]).astype(jnp.int32), axis=1)
    return jnp.where(positions >= 0, count, -1).astype(jnp.int32)


def ssd_local(xs, step, b_in, c_in, rate, docs, doc_before, span):
    length = xs.shape[0]
    heads = step.shape[1]
    width = xs.shape[1] // heads
    count = length // span
    decay = -rate[None, :] * step
    cumul = jnp.cumsum(decay, axis=0)
    base = jnp.concatenate([jnp.zeros((1, heads), cumul.dtype), cumul[span - 1::span][:-1]], axis=0)
    doc_prev = jnp.concatenate([jnp.reshape(doc_before, (1,)).astype(jnp.int32), docs[span - 1::span][:-1].astype(jnp.int32)], axis=0)
    x_blocks = jnp.reshape(xs.astype(cumul.dtype), (count, span, heads, width))
    hp = lax.Precision.HIGHEST
    order = jnp.arange(span)
    lower = order[None, :] <= order[:, None]

    def advance(state, pieces):
        x_c, dt_c, b_c, c_c, cum_c, doc_c, base_c, prev_c = pieces
        rel = cum_c - base_c[None, :]
        gram = jnp.dot(c_c, b_c.T, preferred_element_type=jnp.float32)
        b_wide = b_c.astype(cumul.dtype)
        c_wide = c_c.astype(cumul.dtype)
        rel_h = rel.T
        diff = rel_h[:, :, None] - rel_h[:, None, :]
        valid = jnp.logical_and(lower, doc_c[:, None] == doc_c[None, :])
        decays = jnp.where(valid[None], jnp.exp(jnp.where(valid[None], diff, 0.0)), 0.0)
        mixing = decays * gram[None] * dt_c.T[:, None, :]
        out = jnp.einsum("hts,shp->thp", mixing, x_c, precision=hp)
        carried = (doc_c == prev_c).astype(cumul.dtype)
        entry = jnp.exp(rel) * carried[:, None]
        out = out + entry[:, :, None] * jnp.einsum("tn,hnp->thp", c_wide, state, precision=hp)
        last = rel[-1]
        same = (doc_c == doc_c[-1]).astype(cumul.dtype)
        factor = jnp.exp(last[None, :] - rel) * same[:, None] * dt_c
        fresh = jnp.einsum("sh,sn,shp->hnp", factor, b_wide, x_c, precision=hp)
        link = jnp.exp(last) * (doc_c[-1] == prev_c).astype(cumul.dtype)
        return link[:, None, None] * state + fresh, out

    start = jnp.zeros((heads, b_in.shape[1], width), cumul.dtype)
    pieces = (x_blocks, jnp.reshape(step, (count, span, heads)),
              jnp.reshape(b_in, (count, span, -1)),
              jnp.reshape(c_in, (count, span, -1)),
              jnp.reshape(cumul, (count, span, heads)), jnp.reshape(docs, (count, span)), base, doc_prev)
    final, outs = lax.scan(advance, start, pieces)
    link_all = jnp.exp(cumul[-1]) * (docs[-1] == doc_before).astype(cumul.dtype)
    return jnp.reshape(outs, (length, heads * width)), final, link_all, cumul


def reference(queries, keys_in, values_in, ssm_input, step_size, in_proj_b, out_proj_c, decay_rate, skip_gain, doc_lengths):
    positions = jnp.arange(TOKENS).astype(jnp.int32)
    docs = doc_of(positions, doc_lengths)
    scale = 1.0 / (ATT_HD ** 0.5)
    window = MOST_DOC + TOK_DEV
    pad_keys = jnp.concatenate([jnp.zeros((MOST_DOC, D_ATT), keys_in.dtype), keys_in], axis=0)
    pad_vals = jnp.concatenate([jnp.zeros((MOST_DOC, D_ATT), values_in.dtype), values_in], axis=0)
    pad_pos = jnp.arange(-MOST_DOC, TOKENS).astype(jnp.int32)
    pad_docs = doc_of(pad_pos, doc_lengths)

    def block(index):
        start = (index * TOK_DEV).astype(jnp.int32)
        q_b = lax.dynamic_slice_in_dim(queries, start, TOK_DEV, 0)
        k_b = lax.dynamic_slice_in_dim(pad_keys, start, window, 0)
        v_b = lax.dynamic_slice_in_dim(pad_vals, start, window, 0)
        qpos = lax.dynamic_slice_in_dim(positions, start, TOK_DEV, 0)
        kpos = lax.dynamic_slice_in_dim(pad_pos, start, window, 0)
        qdoc = lax.dynamic_slice_in_dim(docs, start, TOK_DEV, 0)
        kdoc = lax.dynamic_slice_in_dim(pad_docs, start, window, 0)
        q3 = jnp.reshape(q_b, (TOK_DEV, ATT_HEADS, ATT_HD)).astype(jnp.float32)
        k3 = jnp.reshape(k_b, (window, ATT_HEADS, ATT_HD)).astype(jnp.float32)
        v3 = jnp.reshape(v_b, (window, ATT_HEADS, ATT_HD)).astype(jnp.float32)
        scores = jnp.einsum("qhd,khd->hqk", q3, k3) * scale
        kept = jnp.logical_and(kdoc[None, :] == qdoc[:, None], kpos[None, :] <= qpos[:, None])
        scores = jnp.where(kept[None], scores, -1e30)
        top = jnp.max(scores, axis=2, keepdims=True)
        weights = jnp.where(kept[None], jnp.exp(scores - top), 0.0)
        total = jnp.sum(weights, axis=2)
        weights_b = weights.astype(jnp.bfloat16).astype(jnp.float32)
        mixed = jnp.einsum("hqk,khd->qhd", weights_b, v3) / total.T[:, :, None]
        return jnp.reshape(mixed, (TOK_DEV, D_ATT)).astype(jnp.bfloat16)

    attn = jnp.reshape(lax.map(block, jnp.arange(N_CTX).astype(jnp.int32)), (TOKENS, D_ATT))
    per_group = M_HEADS // M_GROUPS
    group_outs = []
    for group in range(M_GROUPS):
        first_head = group * per_group
        outs, final, link_all, cumul = ssd_local(
            ssm_input[:, first_head * M_HD:(first_head + per_group) * M_HD],
            step_size[:, first_head:first_head + per_group],
            in_proj_b[:, group * M_STATE:(group + 1) * M_STATE],
            out_proj_c[:, group * M_STATE:(group + 1) * M_STATE],
            decay_rate[first_head:first_head + per_group],
            docs, jnp.int32(-1), SCAN_LEN)
        group_outs.append(outs)
    outs = jnp.concatenate(group_outs, axis=1)
    skip = jnp.repeat(skip_gain, M_HD)
    ssm = (outs + skip[None, :] * ssm_input.astype(jnp.float32)).astype(jnp.bfloat16)
    return attn, ssm
```

```python
import functools

import jax
import jax.numpy as jnp
from jax import lax
from jax.experimental import pallas as pl
from jax.experimental.pallas import tpu as pltpu
from jax.sharding import Mesh
from jax.sharding import PartitionSpec as P

ATT_HD = 224
M_HD = 64
M_GROUPS = 2
MOST_DOC = 1536
BLOCK = 128
TILE = 256
PLANE = ("x", "c", "y")
CTX = ("z", "x", "c")

F32 = jnp.float32
BF16 = jnp.bfloat16


def compiler_params(mib=48):
    return pltpu.CompilerParams(vmem_limit_bytes=mib * 1024 * 1024)


def split2(value):
    high = value.astype(BF16)
    return high, (value - high.astype(F32)).astype(BF16)


def split3(value):
    high, rest = value.astype(BF16), None
    rest = value - high.astype(F32)
    middle = rest.astype(BF16)
    return high, middle, (rest - middle.astype(F32)).astype(BF16)


def dot(a, b):
    return jnp.dot(a, b, preferred_element_type=F32)


def turn_kernel(count, parts, *refs):
    sources, out, held, turned = refs[:count], refs[count], refs[count + 1 : 2 * count + 1], refs[2 * count + 1]
    in_sems, out_sems = refs[2 * count + 2 :]
    step = turned.shape[0] // parts
    width = step * ATT_HD

    def arriving(i, part):
        columns = pl.ds(part * width, width)
        return pltpu.make_async_copy(sources[i].at[:, columns], held[i].at[:, columns], in_sems.at[i, part])

    def leaving(part):
        rows = pl.ds(part * step, step)
        return pltpu.make_async_copy(turned.at[rows], out.at[rows], out_sems.at[part])

    for part in range(parts):
        for i in range(count):
            arriving(i, part).start()
    for part in range(parts):
        for i in range(count):
            arriving(i, part).wait()
            block = held[i][:, part * width : (part + 1) * width].T
            turned[part * step : (part + 1) * step, i * ATT_HD : (i + 1) * ATT_HD, :] = jnp.reshape(
                block, (step, ATT_HD, BLOCK)
            )
        leaving(part).start()
    for part in range(parts):
        leaving(part).wait()


def turn(arrays, mib):
    count, parts = len(arrays), 4
    width = arrays[0].shape[1]
    heads = width // ATT_HD
    return pl.pallas_call(
        functools.partial(turn_kernel, count, parts),
        in_specs=[pl.BlockSpec(memory_space=pl.ANY)] * count,
        out_specs=pl.BlockSpec(memory_space=pl.ANY),
        out_shape=jax.ShapeDtypeStruct((heads, count * ATT_HD, BLOCK), BF16),
        scratch_shapes=[pltpu.VMEM((BLOCK, width), BF16)] * count
        + [
            pltpu.VMEM((heads, count * ATT_HD, BLOCK), BF16),
            pltpu.SemaphoreType.DMA((count, parts)),
            pltpu.SemaphoreType.DMA((parts,)),
        ],
        compiler_params=compiler_params(mib),
        cost_estimate=pl.CostEstimate(flops=0, bytes_accessed=4 * BLOCK * width * count, transcendentals=0),
    )(*arrays)


def turn_back_kernel(a_ref, out_ref):
    heads = a_ref.shape[0]
    out_ref[...] = jnp.reshape(a_ref[...], (heads * ATT_HD, BLOCK)).T


def turn_back(blocks):
    heads = blocks.shape[0]
    step = 16
    return pl.pallas_call(
        turn_back_kernel,
        grid=(heads // step,),
        in_specs=[pl.BlockSpec((step, ATT_HD, BLOCK), lambda i: (i, 0, 0))],
        out_specs=pl.BlockSpec((BLOCK, step * ATT_HD), lambda i: (0, i)),
        out_shape=jax.ShapeDtypeStruct((BLOCK, heads * ATT_HD), BF16),
        compiler_params=compiler_params(),
        cost_estimate=pl.CostEstimate(flops=0, bytes_accessed=4 * BLOCK * heads * ATT_HD, transcendentals=0),
    )(blocks)


def key_rows_kernel(k_ref, out_ref):
    for i in range(k_ref.shape[0]):
        out_ref[i * BLOCK : (i + 1) * BLOCK, :] = k_ref[i].T


def key_rows(kv_blocks):
    count = kv_blocks.shape[0]
    step = 4
    return pl.pallas_call(
        key_rows_kernel,
        grid=(count // step,),
        in_specs=[pl.BlockSpec((step, ATT_HD, BLOCK), lambda i: (i, 0, 0))],
        out_specs=pl.BlockSpec((step * BLOCK, ATT_HD), lambda i: (i, 0)),
        out_shape=jax.ShapeDtypeStruct((count * BLOCK, ATT_HD), BF16),
        compiler_params=compiler_params(16),
        cost_estimate=pl.CostEstimate(flops=0, bytes_accessed=4 * count * BLOCK * ATT_HD, transcendentals=0),
    )(kv_blocks)


def attend_kernel(
    most, reach_ref, starts_ref, q_ref, own_k, own_v, halo_k, halo_v, o_ref,
    k_rows, v_cols, q_own, o_own, halo_sems, sems, out_sems,
):
    halo = halo_v.shape[0]
    own = q_ref.shape[0]
    per = TILE // BLOCK
    pairs = own // per // 2
    span = 2 * per

    def arriving(p):
        blocks = pl.ds(span * p, span)
        tokens = span * BLOCK
        return (
            pltpu.make_async_copy(
                own_k.at[pl.ds(pl.multiple_of(p * tokens, tokens), tokens)],
                k_rows.at[pl.ds(pl.multiple_of(halo * BLOCK + p * tokens, tokens), tokens)],
                sems.at[0, p],
            ),
            pltpu.make_async_copy(own_v.at[blocks], v_cols.at[pl.ds(halo + span * p, span)], sems.at[1, p]),
            pltpu.make_async_copy(q_ref.at[blocks], q_own.at[blocks], sems.at[2, p]),
        )

    halo_copies = (
        pltpu.make_async_copy(halo_k, k_rows.at[pl.ds(0, halo * BLOCK)], halo_sems.at[0]),
        pltpu.make_async_copy(halo_v, v_cols.at[pl.ds(0, halo)], halo_sems.at[1]),
    )
    for copy in halo_copies:
        copy.start()

    def begin(p, _):
        for copy in arriving(p):
            copy.start()
        return 0

    lax.fori_loop(0, pairs, begin, 0)
    for copy in halo_copies:
        copy.wait()
    factor = 1.4426950408889634 / ATT_HD**0.5
    down = lax.broadcasted_iota(jnp.int32, (TILE, TILE), 0)
    causal = down <= lax.broadcasted_iota(jnp.int32, (TILE, TILE), 1)

    def out_copy(p):
        blocks = pl.ds(2 * per * p, 2 * per)
        return pltpu.make_async_copy(o_own.at[blocks], o_ref.at[blocks], out_sems.at[p])

    def pair(p, _):
        reach = reach_ref[p]
        for copy in arriving(p):
            copy.wait()

        def attend_over(reach):
            first = 2 * p + halo // per + 1 - reach
            rows = pl.multiple_of(first * TILE, TILE)
            for half in range(2):
                j = 2 * p + half
                count = reach + half
                q_t = jnp.concatenate([q_own[per * j + i] for i in range(per)], axis=1)
                start = starts_ref[j]
                scores = []
                for i in range(count):
                    s = dot(k_rows[pl.ds(rows + i * TILE, TILE), :], q_t)
                    kept = down >= start - (j - count + 1 + i) * TILE
                    if i == count - 1:
                        kept = jnp.logical_and(kept, causal)
                    scores.append(jnp.where(kept, s, -1e30))
                top = scores[0]
                for s in scores[1:]:
                    top = jnp.maximum(top, s)
                top = jnp.max(top, axis=0, keepdims=True)
                total = jnp.zeros((TILE, TILE), F32)
                mixed = jnp.zeros((ATT_HD, TILE), F32)
                for i in range(count):
                    weights = jnp.exp2((scores[i] - top) * factor)
                    total = total + weights
                    v_t = jnp.concatenate([v_cols[first * per + i * per + b] for b in range(per)], axis=1)
                    mixed = mixed + dot(v_t, weights.astype(BF16))
                total = jnp.sum(total, axis=0, keepdims=True)
                out = (mixed * (1.0 / total)).astype(BF16)
                for b in range(per):
                    o_own[per * j + b] = out[:, b * BLOCK : (b + 1) * BLOCK]

        for count in range(1, most + 1):
            pl.when(reach == count)(functools.partial(attend_over, count))
        out_copy(p).start()
        return 0

    lax.fori_loop(0, pairs, pair, 0)

    def finish(p, _):
        out_copy(p).wait()
        return 0

    lax.fori_loop(0, pairs, finish, 0)


def attend(q_blocks, own_rows, own_v, halo_rows, halo_v, starts):
    own = own_v.shape[0]
    halo = halo_v.shape[0]
    per = TILE // BLOCK
    tiles = own // per
    most = halo // per + 1
    by_tile = jnp.reshape(starts, (tiles, 1, TILE))
    reach = jnp.arange(0, tiles, 2, dtype=jnp.int32) - by_tile[::2, 0, 0] // TILE + 1
    vmem = pl.BlockSpec(memory_space=pltpu.VMEM)
    anywhere = pl.BlockSpec(memory_space=pl.ANY)
    return pl.pallas_call(
        functools.partial(attend_kernel, most),
        in_specs=[pl.BlockSpec(memory_space=pltpu.SMEM), vmem] + [anywhere] * 5,
        out_specs=anywhere,
        out_shape=jax.ShapeDtypeStruct((own, ATT_HD, BLOCK), BF16),
        scratch_shapes=[
            pltpu.VMEM(((own + halo) * BLOCK, ATT_HD), BF16),
            pltpu.VMEM((own + halo, ATT_HD, BLOCK), BF16),
            pltpu.VMEM((own, ATT_HD, BLOCK), BF16),
            pltpu.VMEM((own, ATT_HD, BLOCK), BF16),
            pltpu.SemaphoreType.DMA((2,)),
            pltpu.SemaphoreType.DMA((3, tiles // 2)),
            pltpu.SemaphoreType.DMA((tiles // 2,)),
        ],
        compiler_params=compiler_params(60),
        cost_estimate=pl.CostEstimate(flops=4_000_000_000, bytes_accessed=8_000_000, transcendentals=4_000_000),
    )(reach, by_tile, q_blocks, own_rows, own_v, halo_rows, halo_v)


def cumulative(rate_ref, step_ref):
    length = step_ref.shape[0]
    decay = -rate_ref[...] * step_ref[...]
    order = lax.broadcasted_iota(jnp.int32, (length, length), 0)
    lower = (lax.broadcasted_iota(jnp.int32, (length, length), 1) <= order).astype(F32).astype(BF16)
    a, b, c = split3(decay)
    return dot(lower, a) + dot(lower, b) + dot(lower, c)


def spread(value, wide_ref):
    return dot(jnp.concatenate(split3(value), axis=1), wide_ref[...])


def state_kernel(first_ref, start_ref, x_ref, step_ref, b_ref, rate_ref, wide_ref, out_ref, weight, passed):
    length = x_ref.shape[0]
    cumul = None

    @pl.when(pl.program_id(0) == 0)
    def _():
        cumul = cumulative(rate_ref, step_ref)
        last = cumul[length - 1 :, :]
        weight[...] = jnp.exp(last - cumul) * step_ref[...]
        linked = jnp.where(start_ref[length - 1 :, :] < first_ref[0], 1.0, 0.0)
        passed[...] = jnp.broadcast_to(jnp.exp(last) * linked, passed.shape)

    last_start = start_ref[length - 1 :, :]
    at = first_ref[0] + lax.broadcasted_iota(jnp.int32, (length, 1), 0)
    same = at >= last_start
    b_same = jnp.where(same, b_ref[...].astype(F32), 0.0).astype(BF16)
    update = spread(weight[...], wide_ref) * x_ref[...].astype(F32)
    high, low = split2(update)
    over = (((0,), (0,)), ((), ()))
    fresh = lax.dot_general(b_same, high, over, preferred_element_type=F32) + lax.dot_general(
        b_same, low, over, preferred_element_type=F32
    )
    states = fresh.shape[0]
    out_ref[:states, :] = fresh
    out_ref[states:, :] = spread(passed[...], wide_ref)


def scan_kernel(
    first_ref, start_ref, x_ref, step_ref, b_ref, c_ref, rate_ref, wide_ref, skip_ref,
    near_ref, far_ref, out_ref, weight, growth, g_high, g_low, c_open,
):
    length = x_ref.shape[0]
    states = b_ref.shape[1]

    @pl.when(pl.program_id(0) == 0)
    def _():
        cumul = cumulative(rate_ref, step_ref)
        growth[...] = jnp.exp(cumul)
        weight[...] = jnp.exp(-cumul) * step_ref[...]
        gram = lax.dot_general(c_ref[...], b_ref[...], (((1,), (1,)), ((), ())), preferred_element_type=F32)
        at = lax.broadcasted_iota(jnp.int32, (length, length), 1)
        kept = jnp.logical_and(
            at <= lax.broadcasted_iota(jnp.int32, (length, length), 0), at + first_ref[0] >= start_ref[...]
        )
        high, low = split2(jnp.where(kept, gram, 0.0))
        g_high[...] = high
        g_low[...] = low
        c_open[...] = jnp.where(start_ref[...] < first_ref[0], c_ref[...].astype(F32), 0.0).astype(BF16)

    x = x_ref[...].astype(F32)
    high, low = split2(spread(weight[...], wide_ref) * x)
    entering = near_ref[:states, :] + near_ref[states : states + 1, :] * far_ref[...]
    e_high, e_low = split2(entering)
    c = c_open[...]
    inner = dot(g_high[...], high) + dot(g_high[...], low) + dot(g_low[...], high) + dot(c, e_high) + dot(c, e_low)
    out_ref[...] = (spread(growth[...], wide_ref) * inner + skip_ref[...] * x).astype(BF16)


def whole(shape):
    return pl.BlockSpec(shape, lambda i: (0,) * len(shape))


def scan_parts(x, step, b_group, c_group, rate, skip, start, first):
    length, width = x.shape
    heads = step.shape[1]
    states = b_group.shape[1]
    chunk = 256
    wide = jnp.repeat(jnp.eye(heads, dtype=BF16), width // heads, axis=1)
    wide = jnp.concatenate([wide] * 3, axis=0)
    rate = rate[None, :]
    start = start[:, None]
    first = jnp.reshape(first, (1,)).astype(jnp.int32)
    smem = pl.BlockSpec(memory_space=pltpu.SMEM)
    columns = lambda rows: pl.BlockSpec((rows, chunk), lambda i: (0, i))
    extra = 8
    state = pl.pallas_call(
        state_kernel,
        grid=(width // chunk,),
        in_specs=[
            smem, whole((length, 1)), columns(length), whole((length, heads)), whole((length, states)),
            whole((1, heads)), columns(3 * heads),
        ],
        out_specs=columns(states + extra),
        out_shape=jax.ShapeDtypeStruct((states + extra, width), F32),
        scratch_shapes=[pltpu.VMEM((length, heads), F32), pltpu.VMEM((extra, heads), F32)],
        compiler_params=compiler_params(16),
        cost_estimate=pl.CostEstimate(flops=2_000_000_000, bytes_accessed=3_000_000, transcendentals=20_000),
    )(first, start, x, step, b_group, rate, wide)

    def finish(near, far):
        return pl.pallas_call(
            scan_kernel,
            grid=(width // chunk,),
            in_specs=[
                smem, whole((length, 1)), columns(length), whole((length, heads)), whole((length, states)),
                whole((length, states)), whole((1, heads)), columns(3 * heads), columns(1),
                columns(states + extra), columns(states),
            ],
            out_specs=columns(length),
            out_shape=jax.ShapeDtypeStruct((length, width), BF16),
            scratch_shapes=[
                pltpu.VMEM((length, heads), F32),
                pltpu.VMEM((length, heads), F32),
                pltpu.VMEM((length, length), BF16),
                pltpu.VMEM((length, length), BF16),
                pltpu.VMEM((length, states), BF16),
            ],
            compiler_params=compiler_params(16),
            cost_estimate=pl.CostEstimate(flops=5_000_000_000, bytes_accessed=6_000_000, transcendentals=40_000),
        )(first, start, x, step, b_group, c_group, rate, wide, jnp.repeat(skip, width // heads)[None, :], near, far)

    return state, finish


def doc_start(positions, doc_lengths):
    begins = jnp.cumsum(doc_lengths) - doc_lengths
    return jnp.max(jnp.where(begins[None, :] <= positions[:, None], begins[None, :], 0), axis=1).astype(jnp.int32)


def exchange(blocks):
    return lax.all_to_all(blocks, PLANE, split_axis=0, concat_axis=0, tiled=True)


def local(
    queries, keys_in, values_in, ssm_input, step_size, in_proj_b, out_proj_c, decay_rate, skip_gain, doc_lengths
):
    together = lax.optimization_barrier
    block_len = ssm_input.shape[0]
    ctx = lax.axis_index(CTX)
    devices = lax.axis_size(CTX)
    planes = lax.axis_size("z")
    plane_tokens = lax.axis_size(PLANE) * BLOCK
    plane_first = lax.axis_index("z") * plane_tokens
    halo_blocks = MOST_DOC // BLOCK
    to_next = [(i, i + 1) for i in range(planes - 1)]
    k = exchange(turn([keys_in], 60))

    first = ctx * block_len
    start = doc_start(first + jnp.arange(block_len), doc_lengths)
    width = in_proj_b.shape[1] // M_GROUPS
    group = lax.axis_index("y") // (lax.axis_size("y") // M_GROUPS)
    b_group = lax.dynamic_slice_in_dim(in_proj_b, group * width, width, 1)
    c_group = lax.dynamic_slice_in_dim(out_proj_c, group * width, width, 1)
    state, finish = scan_parts(ssm_input, step_size, b_group, c_group, decay_rate, skip_gain, start, first)
    starts = doc_start(plane_first + jnp.arange(plane_tokens), doc_lengths) - plane_first
    v_blocks, state, starts = together((turn([values_in], 16), state, starts))

    v = exchange(v_blocks)
    near = lax.ppermute(state, CTX, [(i, i + 1) for i in range(devices - 1)])
    two = state[:width] + state[width : width + 1] * near[:width]
    halo_k = lax.ppermute(k[-halo_blocks:], "z", to_next)
    own_rows = key_rows(k)
    halo_rows = key_rows(halo_k)
    q_blocks, own_rows, halo_rows = together((turn([queries], 16), own_rows, halo_rows))

    q = exchange(q_blocks)
    halo_v = lax.ppermute(v[-halo_blocks:], "z", to_next)
    q, halo_v, two = together((q, halo_v, two))

    far = lax.ppermute(two, CTX, [(i, i + 2) for i in range(devices - 2)])
    o_blocks, far = together((attend(q, own_rows, v, halo_rows, halo_v, starts), far))

    return turn_back(exchange(o_blocks)), finish(near, far)


def solution(mesh):
    ctx, head = mesh.devices.shape
    inner = Mesh(mesh.devices.reshape(4, ctx // 8, 2, head), ("z", "x", "c", "y"))
    everywhere = P(("z", "x", "c", "y"), None)
    return jax.shard_map(
        local,
        mesh=inner,
        in_specs=(
            everywhere, everywhere, everywhere,
            P(CTX, "y"), P(CTX, "y"), P(CTX, None), P(CTX, None), P("y"), P("y"), P(),
        ),
        out_specs=(everywhere, P(CTX, "y")),
        check_vma=False,
    )
```

```python
import functools

import jax
import jax.numpy as jnp
from jax import lax
from jax.experimental import pallas as pl
from jax.experimental.pallas import tpu as pltpu
from jax.sharding import Mesh
from jax.sharding import PartitionSpec as P

ATT_HD = 224
M_HD = 64
M_GROUPS = 2
MOST_DOC = 1536
BLOCK = 128
TILE = 256
PLANE = ("x", "c", "y")
CTX = ("z", "x", "c")

F32 = jnp.float32
BF16 = jnp.bfloat16


def compiler_params(mib=48):
    return pltpu.CompilerParams(vmem_limit_bytes=mib * 1024 * 1024)


def split2(value):
    high = value.astype(BF16)
    return high, (value - high.astype(F32)).astype(BF16)


def split3(value):
    high, rest = value.astype(BF16), None
    rest = value - high.astype(F32)
    middle = rest.astype(BF16)
    return high, middle, (rest - middle.astype(F32)).astype(BF16)


def dot(a, b):
    return jnp.dot(a, b, preferred_element_type=F32)


def turn_kernel(count, parts, *refs):
    sources, out, held, turned = refs[:count], refs[count], refs[count + 1 : 2 * count + 1], refs[2 * count + 1]
    in_sems, out_sems = refs[2 * count + 2 :]
    step = turned.shape[0] // parts
    width = step * ATT_HD

    def arriving(i, part):
        columns = pl.ds(part * width, width)
        return pltpu.make_async_copy(sources[i].at[:, columns], held[i].at[:, columns], in_sems.at[i, part])

    def leaving(part):
        rows = pl.ds(part * step, step)
        return pltpu.make_async_copy(turned.at[rows], out.at[rows], out_sems.at[part])

    for part in range(parts):
        for i in range(count):
            arriving(i, part).start()
    for part in range(parts):
        for i in range(count):
            arriving(i, part).wait()
            block = held[i][:, part * width : (part + 1) * width].T
            turned[part * step : (part + 1) * step, i * ATT_HD : (i + 1) * ATT_HD, :] = jnp.reshape(
                block, (step, ATT_HD, BLOCK)
            )
        leaving(part).start()
    for part in range(parts):
        leaving(part).wait()


def turn(arrays, mib):
    count, parts = len(arrays), 4
    width = arrays[0].shape[1]
    heads = width // ATT_HD
    return pl.pallas_call(
        functools.partial(turn_kernel, count, parts),
        in_specs=[pl.BlockSpec(memory_space=pl.ANY)] * count,
        out_specs=pl.BlockSpec(memory_space=pl.ANY),
        out_shape=jax.ShapeDtypeStruct((heads, count * ATT_HD, BLOCK), BF16),
        scratch_shapes=[pltpu.VMEM((BLOCK, width), BF16)] * count
        + [
            pltpu.VMEM((heads, count * ATT_HD, BLOCK), BF16),
            pltpu.SemaphoreType.DMA((count, parts)),
            pltpu.SemaphoreType.DMA((parts,)),
        ],
        compiler_params=compiler_params(mib),
        cost_estimate=pl.CostEstimate(flops=0, bytes_accessed=4 * BLOCK * width * count, transcendentals=0),
    )(*arrays)


def turn_back_kernel(a_ref, out_ref):
    heads = a_ref.shape[0]
    out_ref[...] = jnp.reshape(a_ref[...], (heads * ATT_HD, BLOCK)).T


def turn_back(blocks):
    heads = blocks.shape[0]
    step = 16
    return pl.pallas_call(
        turn_back_kernel,
        grid=(heads // step,),
        in_specs=[pl.BlockSpec((step, ATT_HD, BLOCK), lambda i: (i, 0, 0))],
        out_specs=pl.BlockSpec((BLOCK, step * ATT_HD), lambda i: (0, i)),
        out_shape=jax.ShapeDtypeStruct((BLOCK, heads * ATT_HD), BF16),
        compiler_params=compiler_params(16),
        cost_estimate=pl.CostEstimate(flops=0, bytes_accessed=4 * BLOCK * heads * ATT_HD, transcendentals=0),
    )(blocks)


def key_rows_kernel(k_ref, out_ref):
    for i in range(k_ref.shape[0]):
        out_ref[i * BLOCK : (i + 1) * BLOCK, :] = k_ref[i].T


def key_rows(kv_blocks):
    count = kv_blocks.shape[0]
    step = 4
    return pl.pallas_call(
        key_rows_kernel,
        grid=(count // step,),
        in_specs=[pl.BlockSpec((step, ATT_HD, BLOCK), lambda i: (i, 0, 0))],
        out_specs=pl.BlockSpec((step * BLOCK, ATT_HD), lambda i: (i, 0)),
        out_shape=jax.ShapeDtypeStruct((count * BLOCK, ATT_HD), BF16),
        compiler_params=compiler_params(16),
        cost_estimate=pl.CostEstimate(flops=0, bytes_accessed=4 * count * BLOCK * ATT_HD, transcendentals=0),
    )(kv_blocks)


def attend_kernel(
    most, reach_ref, starts_ref, q_ref, own_k, own_v, halo_k, halo_v, o_ref,
    k_rows, v_cols, q_own, o_own, halo_sems, sems, out_sems,
):
    halo = halo_v.shape[0]
    own = q_ref.shape[0]
    per = TILE // BLOCK
    pairs = own // per // 2
    span = 2 * per

    def arriving(p):
        blocks = pl.ds(span * p, span)
        tokens = span * BLOCK
        return (
            pltpu.make_async_copy(
                own_k.at[pl.ds(pl.multiple_of(p * tokens, tokens), tokens)],
                k_rows.at[pl.ds(pl.multiple_of(halo * BLOCK + p * tokens, tokens), tokens)],
                sems.at[0, p],
            ),
            pltpu.make_async_copy(own_v.at[blocks], v_cols.at[pl.ds(halo + span * p, span)], sems.at[1, p]),
            pltpu.make_async_copy(q_ref.at[blocks], q_own.at[blocks], sems.at[2, p]),
        )

    halo_copies = (
        pltpu.make_async_copy(halo_k, k_rows.at[pl.ds(0, halo * BLOCK)], halo_sems.at[0]),
        pltpu.make_async_copy(halo_v, v_cols.at[pl.ds(0, halo)], halo_sems.at[1]),
    )
    for copy in halo_copies:
        copy.start()

    def begin(p, _):
        for copy in arriving(p):
            copy.start()
        return 0

    lax.fori_loop(0, pairs, begin, 0)
    for copy in halo_copies:
        copy.wait()
    factor = 1.4426950408889634 / ATT_HD**0.5
    down = lax.broadcasted_iota(jnp.int32, (TILE, TILE), 0)
    causal = down <= lax.broadcasted_iota(jnp.int32, (TILE, TILE), 1)

    def out_copy(p):
        blocks = pl.ds(2 * per * p, 2 * per)
        return pltpu.make_async_copy(o_own.at[blocks], o_ref.at[blocks], out_sems.at[p])

    def pair(p, _):
        reach = reach_ref[p]
        for copy in arriving(p):
            copy.wait()

        def attend_over(reach):
            first = 2 * p + halo // per + 1 - reach
            rows = pl.multiple_of(first * TILE, TILE)
            starts = [starts_ref[2 * p + half] for half in range(2)]
            queries = [
                jnp.concatenate([q_own[per * (2 * p + half) + i] for i in range(per)], axis=1) for half in range(2)
            ]
            counts = [reach, reach + 1]

            def score(half, i):
                s = dot(k_rows[pl.ds(rows + i * TILE, TILE), :], queries[half])
                kept = down >= starts[half] - (2 * p + half - counts[half] + 1 + i) * TILE
                if i == counts[half] - 1:
                    kept = jnp.logical_and(kept, causal)
                return jnp.where(kept, s, -1e30)

            def peak(scores):
                tops = [jnp.max(jnp.reshape(s, (TILE // 8, 8, TILE)), axis=0) for s in scores]
                return jnp.max(functools.reduce(jnp.maximum, tops), axis=0, keepdims=True)

            def values(i):
                return jnp.concatenate([v_cols[first * per + i * per + b] for b in range(per)], axis=1)

            def put(half, mixed, total):
                out = (mixed * (1.0 / jnp.sum(total, axis=0, keepdims=True))).astype(BF16)
                for b in range(per):
                    o_own[per * (2 * p + half) + b] = out[:, b * BLOCK : (b + 1) * BLOCK]

            def weigh(s, top, total):
                weights = jnp.exp2((s - top) * factor)
                return weights.astype(BF16), total + jnp.sum(jnp.reshape(weights, (TILE // 8, 8, TILE)), axis=0)

            total = [jnp.zeros((8, TILE), F32)] * 2
            mixed = [jnp.zeros((ATT_HD, TILE), F32)] * 2
            near_scores = [score(0, i) for i in range(counts[0])]
            near_top = peak(near_scores)
            near_weights, scores = [], []
            for i in range(counts[1]):
                scores.append(score(1, i))
                if i < counts[0]:
                    weights, total[0] = weigh(near_scores[i], near_top, total[0])
                    near_weights.append(weights)
            top = peak(scores)
            last = None
            for i in range(counts[1]):
                if i < counts[0]:
                    mixed[0] = mixed[0] + dot(values(i), near_weights[i])
                weights, total[1] = weigh(scores[i], top, total[1])
                if last is not None:
                    mixed[1] = mixed[1] + dot(values(i - 1), last)
                last = weights
            put(0, mixed[0], total[0])
            mixed[1] = mixed[1] + dot(values(counts[1] - 1), last)
            put(1, mixed[1], total[1])

        for count in range(1, most + 1):
            pl.when(reach == count)(functools.partial(attend_over, count))
        out_copy(p).start()
        return 0

    lax.fori_loop(0, pairs, pair, 0)

    def finish(p, _):
        out_copy(p).wait()
        return 0

    lax.fori_loop(0, pairs, finish, 0)


def attend(q_blocks, own_rows, own_v, halo_rows, halo_v, starts):
    own = own_v.shape[0]
    halo = halo_v.shape[0]
    per = TILE // BLOCK
    tiles = own // per
    most = halo // per + 1
    by_tile = jnp.reshape(starts, (tiles, 1, TILE))
    reach = jnp.arange(0, tiles, 2, dtype=jnp.int32) - by_tile[::2, 0, 0] // TILE + 1
    vmem = pl.BlockSpec(memory_space=pltpu.VMEM)
    anywhere = pl.BlockSpec(memory_space=pl.ANY)
    return pl.pallas_call(
        functools.partial(attend_kernel, most),
        in_specs=[pl.BlockSpec(memory_space=pltpu.SMEM), vmem] + [anywhere] * 5,
        out_specs=anywhere,
        out_shape=jax.ShapeDtypeStruct((own, ATT_HD, BLOCK), BF16),
        scratch_shapes=[
            pltpu.VMEM(((own + halo) * BLOCK, ATT_HD), BF16),
            pltpu.VMEM((own + halo, ATT_HD, BLOCK), BF16),
            pltpu.VMEM((own, ATT_HD, BLOCK), BF16),
            pltpu.VMEM((own, ATT_HD, BLOCK), BF16),
            pltpu.SemaphoreType.DMA((2,)),
            pltpu.SemaphoreType.DMA((3, tiles // 2)),
            pltpu.SemaphoreType.DMA((tiles // 2,)),
        ],
        compiler_params=compiler_params(60),
        cost_estimate=pl.CostEstimate(flops=1_000_000, bytes_accessed=1_000_000, transcendentals=0),
    )(reach, by_tile, q_blocks, own_rows, own_v, halo_rows, halo_v)


def cumulative(rate_ref, step_ref):
    length = step_ref.shape[0]
    decay = -rate_ref[...] * step_ref[...]
    order = lax.broadcasted_iota(jnp.int32, (length, length), 0)
    lower = (lax.broadcasted_iota(jnp.int32, (length, length), 1) <= order).astype(F32).astype(BF16)
    a, b, c = split3(decay)
    return dot(lower, a) + dot(lower, b) + dot(lower, c)


def spread(value, wide_ref):
    return dot(jnp.concatenate(split3(value), axis=1), wide_ref[...])


def state_kernel(first_ref, start_ref, x_ref, step_ref, b_ref, rate_ref, wide_ref, out_ref, weight, passed):
    length = x_ref.shape[0]
    cumul = None

    @pl.when(pl.program_id(0) == 0)
    def _():
        cumul = cumulative(rate_ref, step_ref)
        last = cumul[length - 1 :, :]
        weight[...] = jnp.exp(last - cumul) * step_ref[...]
        linked = jnp.where(start_ref[length - 1 :, :] < first_ref[0], 1.0, 0.0)
        passed[...] = jnp.broadcast_to(jnp.exp(last) * linked, passed.shape)

    last_start = start_ref[length - 1 :, :]
    at = first_ref[0] + lax.broadcasted_iota(jnp.int32, (length, 1), 0)
    same = at >= last_start
    b_same = jnp.where(same, b_ref[...].astype(F32), 0.0).astype(BF16)
    update = spread(weight[...], wide_ref) * x_ref[...].astype(F32)
    high, low = split2(update)
    over = (((0,), (0,)), ((), ()))
    fresh = lax.dot_general(b_same, high, over, preferred_element_type=F32) + lax.dot_general(
        b_same, low, over, preferred_element_type=F32
    )
    states = fresh.shape[0]
    out_ref[:states, :] = fresh
    out_ref[states:, :] = spread(passed[...], wide_ref)


def scan_kernel(
    first_ref, start_ref, x_ref, step_ref, b_ref, c_ref, rate_ref, wide_ref, skip_ref,
    near_ref, far_ref, out_ref, weight, growth, g_high, g_low, c_open,
):
    length = x_ref.shape[0]
    states = b_ref.shape[1]

    @pl.when(pl.program_id(0) == 0)
    def _():
        cumul = cumulative(rate_ref, step_ref)
        growth[...] = jnp.exp(cumul)
        weight[...] = jnp.exp(-cumul) * step_ref[...]
        gram = lax.dot_general(c_ref[...], b_ref[...], (((1,), (1,)), ((), ())), preferred_element_type=F32)
        at = lax.broadcasted_iota(jnp.int32, (length, length), 1)
        kept = jnp.logical_and(
            at <= lax.broadcasted_iota(jnp.int32, (length, length), 0), at + first_ref[0] >= start_ref[...]
        )
        high, low = split2(jnp.where(kept, gram, 0.0))
        g_high[...] = high
        g_low[...] = low
        c_open[...] = jnp.where(start_ref[...] < first_ref[0], c_ref[...].astype(F32), 0.0).astype(BF16)

    x = x_ref[...].astype(F32)
    high, low = split2(spread(weight[...], wide_ref) * x)
    entering = near_ref[:states, :] + near_ref[states : states + 1, :] * far_ref[...]
    e_high, e_low = split2(entering)
    c = c_open[...]
    inner = dot(g_high[...], high) + dot(g_high[...], low) + dot(g_low[...], high) + dot(c, e_high) + dot(c, e_low)
    out_ref[...] = (spread(growth[...], wide_ref) * inner + skip_ref[...] * x).astype(BF16)


def whole(shape):
    return pl.BlockSpec(shape, lambda i: (0,) * len(shape))


def scan_parts(x, step, b_group, c_group, rate, skip, start, first):
    length, width = x.shape
    heads = step.shape[1]
    states = b_group.shape[1]
    chunk = 256
    wide = jnp.repeat(jnp.eye(heads, dtype=BF16), width // heads, axis=1)
    wide = jnp.concatenate([wide] * 3, axis=0)
    rate = rate[None, :]
    start = start[:, None]
    first = jnp.reshape(first, (1,)).astype(jnp.int32)
    smem = pl.BlockSpec(memory_space=pltpu.SMEM)
    columns = lambda rows: pl.BlockSpec((rows, chunk), lambda i: (0, i))
    extra = 8
    state = pl.pallas_call(
        state_kernel,
        grid=(width // chunk,),
        in_specs=[
            smem, whole((length, 1)), columns(length), whole((length, heads)), whole((length, states)),
            whole((1, heads)), columns(3 * heads),
        ],
        out_specs=columns(states + extra),
        out_shape=jax.ShapeDtypeStruct((states + extra, width), F32),
        scratch_shapes=[pltpu.VMEM((length, heads), F32), pltpu.VMEM((extra, heads), F32)],
        compiler_params=compiler_params(16),
        cost_estimate=pl.CostEstimate(flops=2_000_000_000, bytes_accessed=3_000_000, transcendentals=20_000),
    )(first, start, x, step, b_group, rate, wide)

    def finish(near, far):
        return pl.pallas_call(
            scan_kernel,
            grid=(width // chunk,),
            in_specs=[
                smem, whole((length, 1)), columns(length), whole((length, heads)), whole((length, states)),
                whole((length, states)), whole((1, heads)), columns(3 * heads), columns(1),
                columns(states + extra), columns(states),
            ],
            out_specs=columns(length),
            out_shape=jax.ShapeDtypeStruct((length, width), BF16),
            scratch_shapes=[
                pltpu.VMEM((length, heads), F32),
                pltpu.VMEM((length, heads), F32),
                pltpu.VMEM((length, length), BF16),
                pltpu.VMEM((length, length), BF16),
                pltpu.VMEM((length, states), BF16),
            ],
            compiler_params=compiler_params(16),
            cost_estimate=pl.CostEstimate(flops=5_000_000_000, bytes_accessed=6_000_000, transcendentals=40_000),
        )(first, start, x, step, b_group, c_group, rate, wide, jnp.repeat(skip, width // heads)[None, :], near, far)

    return state, finish


def doc_start(positions, doc_lengths):
    begins = jnp.cumsum(doc_lengths) - doc_lengths
    return jnp.max(jnp.where(begins[None, :] <= positions[:, None], begins[None, :], 0), axis=1).astype(jnp.int32)


def exchange(blocks):
    return lax.all_to_all(blocks, PLANE, split_axis=0, concat_axis=0, tiled=True)


def local(
    queries, keys_in, values_in, ssm_input, step_size, in_proj_b, out_proj_c, decay_rate, skip_gain, doc_lengths
):
    together = lax.optimization_barrier
    block_len = ssm_input.shape[0]
    ctx = lax.axis_index(CTX)
    devices = lax.axis_size(CTX)
    planes = lax.axis_size("z")
    plane_tokens = lax.axis_size(PLANE) * BLOCK
    plane_first = lax.axis_index("z") * plane_tokens
    halo_blocks = MOST_DOC // BLOCK
    to_next = [(i, i + 1) for i in range(planes - 1)]
    k = exchange(turn([keys_in], 60))

    first = ctx * block_len
    start = doc_start(first + jnp.arange(block_len), doc_lengths)
    width = in_proj_b.shape[1] // M_GROUPS
    group = lax.axis_index("y") // (lax.axis_size("y") // M_GROUPS)
    b_group = lax.dynamic_slice_in_dim(in_proj_b, group * width, width, 1)
    c_group = lax.dynamic_slice_in_dim(out_proj_c, group * width, width, 1)
    state, finish = scan_parts(ssm_input, step_size, b_group, c_group, decay_rate, skip_gain, start, first)
    starts = doc_start(plane_first + jnp.arange(plane_tokens), doc_lengths) - plane_first
    values_in, state = together((values_in, state))
    near = lax.ppermute(state, CTX, [(i, i + 1) for i in range(devices - 1)])
    v_blocks, near, starts = together((turn([values_in], 16), near, starts))

    v = exchange(v_blocks)
    halo_k = lax.ppermute(k[-halo_blocks:], "z", to_next)
    own_rows = key_rows(k)
    halo_rows = key_rows(halo_k)
    two = state[:width] + state[width : width + 1] * near[:width]
    q_blocks, own_rows, halo_rows, two = together((turn([queries], 16), own_rows, halo_rows, two))

    q = exchange(q_blocks)
    halo_v = lax.ppermute(v[-halo_blocks:], "z", to_next)
    q, halo_v = together((q, halo_v))

    far = lax.ppermute(two, CTX, [(i, i + 2) for i in range(devices - 2)])
    o_blocks, far = together((attend(q, own_rows, v, halo_rows, halo_v, starts), far))

    return turn_back(exchange(o_blocks)), finish(near, far)


def solution(mesh):
    ctx, head = mesh.devices.shape
    inner = Mesh(mesh.devices.reshape(4, ctx // 8, 2, head), ("z", "x", "c", "y"))
    everywhere = P(("z", "x", "c", "y"), None)
    return jax.shard_map(
        local,
        mesh=inner,
        in_specs=(
            everywhere, everywhere, everywhere,
            P(CTX, "y"), P(CTX, "y"), P(CTX, None), P(CTX, None), P("y"), P("y"), P(),
        ),
        out_specs=(everywhere, P(CTX, "y")),
        check_vma=False,
    )
```

```python
import functools

import jax
import jax.numpy as jnp
from jax import lax
from jax.experimental import pallas as pl
from jax.experimental.pallas import tpu as pltpu
from jax.sharding import Mesh
from jax.sharding import PartitionSpec as P

ATT_HD = 224
M_HD = 64
M_GROUPS = 2
MOST_DOC = 1536
BLOCK = 128
TILE = 256
GROUP = 2
PLANE = ("x", "c", "y")
CTX = ("z", "x", "c")

F32 = jnp.float32
BF16 = jnp.bfloat16


def compiler_params(mib=48):
    return pltpu.CompilerParams(vmem_limit_bytes=mib * 1024 * 1024)


def split2(value):
    high = value.astype(BF16)
    return high, (value - high.astype(F32)).astype(BF16)


def split3(value):
    high, rest = value.astype(BF16), None
    rest = value - high.astype(F32)
    middle = rest.astype(BF16)
    return high, middle, (rest - middle.astype(F32)).astype(BF16)


def dot(a, b):
    return jnp.dot(a, b, preferred_element_type=F32)


def turn_kernel(count, parts, *refs):
    sources, out, held, turned = refs[:count], refs[count], refs[count + 1 : 2 * count + 1], refs[2 * count + 1]
    in_sems, out_sems = refs[2 * count + 2 :]
    step = turned.shape[0] // parts
    width = step * ATT_HD

    def arriving(i, part):
        columns = pl.ds(part * width, width)
        return pltpu.make_async_copy(sources[i].at[:, columns], held[i].at[:, columns], in_sems.at[i, part])

    def leaving(part):
        rows = pl.ds(part * step, step)
        return pltpu.make_async_copy(turned.at[rows], out.at[rows], out_sems.at[part])

    for part in range(parts):
        for i in range(count):
            arriving(i, part).start()
    for part in range(parts):
        for i in range(count):
            arriving(i, part).wait()
            block = held[i][:, part * width : (part + 1) * width].T
            turned[part * step : (part + 1) * step, i * ATT_HD : (i + 1) * ATT_HD, :] = jnp.reshape(
                block, (step, ATT_HD, BLOCK)
            )
        leaving(part).start()
    for part in range(parts):
        leaving(part).wait()


def turn(arrays, mib):
    count, parts = len(arrays), 4
    width = arrays[0].shape[1]
    heads = width // ATT_HD
    return pl.pallas_call(
        functools.partial(turn_kernel, count, parts),
        in_specs=[pl.BlockSpec(memory_space=pl.ANY)] * count,
        out_specs=pl.BlockSpec(memory_space=pl.ANY),
        out_shape=jax.ShapeDtypeStruct((heads, count * ATT_HD, BLOCK), BF16),
        scratch_shapes=[pltpu.VMEM((BLOCK, width), BF16)] * count
        + [
            pltpu.VMEM((heads, count * ATT_HD, BLOCK), BF16),
            pltpu.SemaphoreType.DMA((count, parts)),
            pltpu.SemaphoreType.DMA((parts,)),
        ],
        compiler_params=compiler_params(mib),
        cost_estimate=pl.CostEstimate(flops=0, bytes_accessed=4 * BLOCK * width * count, transcendentals=0),
    )(*arrays)


def turn_back_kernel(a_ref, out_ref):
    heads = a_ref.shape[0]
    out_ref[...] = jnp.reshape(a_ref[...], (heads * ATT_HD, BLOCK)).T


def turn_back(blocks):
    heads = blocks.shape[0]
    step = 16
    return pl.pallas_call(
        turn_back_kernel,
        grid=(heads // step,),
        in_specs=[pl.BlockSpec((step, ATT_HD, BLOCK), lambda i: (i, 0, 0))],
        out_specs=pl.BlockSpec((BLOCK, step * ATT_HD), lambda i: (0, i)),
        out_shape=jax.ShapeDtypeStruct((BLOCK, heads * ATT_HD), BF16),
        compiler_params=compiler_params(16),
        cost_estimate=pl.CostEstimate(flops=0, bytes_accessed=4 * BLOCK * heads * ATT_HD, transcendentals=0),
    )(blocks)


def key_rows_kernel(k_ref, out_ref):
    for i in range(k_ref.shape[0]):
        out_ref[i * BLOCK : (i + 1) * BLOCK, :] = k_ref[i].T


def key_rows(kv_blocks):
    count = kv_blocks.shape[0]
    step = 4
    return pl.pallas_call(
        key_rows_kernel,
        grid=(count // step,),
        in_specs=[pl.BlockSpec((step, ATT_HD, BLOCK), lambda i: (i, 0, 0))],
        out_specs=pl.BlockSpec((step * BLOCK, ATT_HD), lambda i: (i, 0)),
        out_shape=jax.ShapeDtypeStruct((count * BLOCK, ATT_HD), BF16),
        compiler_params=compiler_params(16),
        cost_estimate=pl.CostEstimate(flops=0, bytes_accessed=4 * count * BLOCK * ATT_HD, transcendentals=0),
    )(kv_blocks)


def attend_kernel(
    most, reach_ref, starts_ref, q_ref, own_k, own_v, halo_k, halo_v, o_ref,
    k_rows, v_cols, q_own, o_own, halo_sems, sems, out_sems,
):
    halo = halo_v.shape[0]
    own = q_ref.shape[0]
    per = TILE // BLOCK
    pairs = own // per // GROUP
    span = GROUP * per

    def arriving(p):
        blocks = pl.ds(span * p, span)
        tokens = span * BLOCK
        return (
            pltpu.make_async_copy(
                own_k.at[pl.ds(pl.multiple_of(p * tokens, tokens), tokens)],
                k_rows.at[pl.ds(pl.multiple_of(halo * BLOCK + p * tokens, tokens), tokens)],
                sems.at[0, p],
            ),
            pltpu.make_async_copy(own_v.at[blocks], v_cols.at[pl.ds(halo + span * p, span)], sems.at[1, p]),
            pltpu.make_async_copy(q_ref.at[blocks], q_own.at[blocks], sems.at[2, p]),
        )

    halo_copies = (
        pltpu.make_async_copy(halo_k, k_rows.at[pl.ds(0, halo * BLOCK)], halo_sems.at[0]),
        pltpu.make_async_copy(halo_v, v_cols.at[pl.ds(0, halo)], halo_sems.at[1]),
    )
    for copy in halo_copies:
        copy.start()

    def begin(p, _):
        for copy in arriving(p):
            copy.start()
        return 0

    lax.fori_loop(0, pairs, begin, 0)
    for copy in halo_copies:
        copy.wait()
    factor = 1.4426950408889634 / ATT_HD**0.5
    down = lax.broadcasted_iota(jnp.int32, (TILE, TILE), 0)
    causal = down <= lax.broadcasted_iota(jnp.int32, (TILE, TILE), 1)

    def out_copy(p):
        blocks = pl.ds(span * p, span)
        return pltpu.make_async_copy(o_own.at[blocks], o_ref.at[blocks], out_sems.at[p])

    def pair(p, _):
        reach = reach_ref[p]
        for copy in arriving(p):
            copy.wait()

        def attend_over(reach):
            first = GROUP * p + halo // per + 1 - reach
            rows = pl.multiple_of(first * TILE, TILE)
            starts = [starts_ref[GROUP * p + part] for part in range(GROUP)]
            counts = [reach + part for part in range(GROUP)]

            def score(part, i):
                s = dot(k_rows[pl.ds(rows + i * TILE, TILE), :], queries)
                kept = down >= starts[part] - (GROUP * p + part - counts[part] + 1 + i) * TILE
                if i == counts[part] - 1:
                    kept = jnp.logical_and(kept, causal)
                return jnp.where(kept, s, -1e30)

            def peak(scores):
                tops = [jnp.max(jnp.reshape(s, (TILE // 8, 8, TILE)), axis=0) for s in scores]
                return jnp.max(functools.reduce(jnp.maximum, tops), axis=0, keepdims=True)

            def values(i):
                return jnp.concatenate([v_cols[first * per + i * per + b] for b in range(per)], axis=1)

            before, top = [], None
            for part in range(GROUP + 1):
                scores, waiting = [], None
                total = jnp.zeros((8, TILE), F32)
                mixed = jnp.zeros((ATT_HD, TILE), F32)
                if part < GROUP:
                    queries = jnp.concatenate([q_own[per * (GROUP * p + part) + b] for b in range(per)], axis=1)
                for i in range(counts[min(part, GROUP - 1)]):
                    if part < GROUP:
                        scores.append(score(part, i))
                    if i < len(before):
                        weights = jnp.exp2((before[i] - top) * factor)
                        total = total + jnp.sum(jnp.reshape(weights, (TILE // 8, 8, TILE)), axis=0)
                        if waiting is not None:
                            mixed = mixed + dot(values(i - 1), waiting)
                        waiting = weights.astype(BF16)
                if part > 0:
                    mixed = mixed + dot(values(len(before) - 1), waiting)
                    out = (mixed * (1.0 / jnp.sum(total, axis=0, keepdims=True))).astype(BF16)
                    for b in range(per):
                        o_own[per * (GROUP * p + part - 1) + b] = out[:, b * BLOCK : (b + 1) * BLOCK]
                if part < GROUP:
                    before, top = scores, peak(scores)

        for count in range(1, most + 1):
            pl.when(reach == count)(functools.partial(attend_over, count))
        out_copy(p).start()
        return 0

    lax.fori_loop(0, pairs, pair, 0)

    def finish(p, _):
        out_copy(p).wait()
        return 0

    lax.fori_loop(0, pairs, finish, 0)


def attend(q_blocks, own_rows, own_v, halo_rows, halo_v, starts):
    own = own_v.shape[0]
    halo = halo_v.shape[0]
    per = TILE // BLOCK
    tiles = own // per
    most = halo // per + 1
    by_tile = jnp.reshape(starts, (tiles, 1, TILE))
    reach = jnp.arange(0, tiles, GROUP, dtype=jnp.int32) - by_tile[::GROUP, 0, 0] // TILE + 1
    vmem = pl.BlockSpec(memory_space=pltpu.VMEM)
    anywhere = pl.BlockSpec(memory_space=pl.ANY)
    return pl.pallas_call(
        functools.partial(attend_kernel, most),
        in_specs=[pl.BlockSpec(memory_space=pltpu.SMEM), vmem] + [anywhere] * 5,
        out_specs=anywhere,
        out_shape=jax.ShapeDtypeStruct((own, ATT_HD, BLOCK), BF16),
        scratch_shapes=[
            pltpu.VMEM(((own + halo) * BLOCK, ATT_HD), BF16),
            pltpu.VMEM((own + halo, ATT_HD, BLOCK), BF16),
            pltpu.VMEM((own, ATT_HD, BLOCK), BF16),
            pltpu.VMEM((own, ATT_HD, BLOCK), BF16),
            pltpu.SemaphoreType.DMA((2,)),
            pltpu.SemaphoreType.DMA((3, tiles // GROUP)),
            pltpu.SemaphoreType.DMA((tiles // GROUP,)),
        ],
        compiler_params=compiler_params(60),
        cost_estimate=pl.CostEstimate(flops=1_000_000, bytes_accessed=1_000_000, transcendentals=0),
    )(reach, by_tile, q_blocks, own_rows, own_v, halo_rows, halo_v)


def cumulative(rate_ref, step_ref):
    length = step_ref.shape[0]
    decay = -rate_ref[...] * step_ref[...]
    order = lax.broadcasted_iota(jnp.int32, (length, length), 0)
    lower = (lax.broadcasted_iota(jnp.int32, (length, length), 1) <= order).astype(F32).astype(BF16)
    a, b, c = split3(decay)
    return dot(lower, a) + dot(lower, b) + dot(lower, c)


def spread(value, wide_ref):
    return dot(jnp.concatenate(split3(value), axis=1), wide_ref[...])


def state_kernel(first_ref, start_ref, x_ref, step_ref, b_ref, rate_ref, wide_ref, upper_ref, lower_ref, weight, passed):
    length = x_ref.shape[0]
    cumul = None

    @pl.when(pl.program_id(0) == 0)
    def _():
        cumul = cumulative(rate_ref, step_ref)
        last = cumul[length - 1 :, :]
        weight[...] = jnp.exp(last - cumul) * step_ref[...]
        linked = jnp.where(start_ref[length - 1 :, :] < first_ref[0], 1.0, 0.0)
        passed[...] = jnp.broadcast_to(jnp.exp(last) * linked, passed.shape)

    last_start = start_ref[length - 1 :, :]
    at = first_ref[0] + lax.broadcasted_iota(jnp.int32, (length, 1), 0)
    same = at >= last_start
    b_same = jnp.where(same, b_ref[...].astype(F32), 0.0).astype(BF16)
    update = spread(weight[...], wide_ref) * x_ref[...].astype(F32)
    high, low = split2(update)
    over = (((0,), (0,)), ((), ()))
    fresh = lax.dot_general(b_same, high, over, preferred_element_type=F32) + lax.dot_general(
        b_same, low, over, preferred_element_type=F32
    )
    half = lower_ref.shape[0]
    upper_ref[:half, :] = fresh[:half]
    upper_ref[half:, :] = spread(passed[...], wide_ref)
    lower_ref[...] = fresh[half:]


def scan_kernel(
    first_ref, start_ref, x_ref, step_ref, b_ref, c_ref, rate_ref, wide_ref, skip_ref,
    upper_ref, lower_ref, far_ref, out_ref, weight, growth, g_high, g_low, c_open,
):
    length = x_ref.shape[0]
    states = b_ref.shape[1]

    @pl.when(pl.program_id(0) == 0)
    def _():
        cumul = cumulative(rate_ref, step_ref)
        growth[...] = jnp.exp(cumul)
        weight[...] = jnp.exp(-cumul) * step_ref[...]
        gram = lax.dot_general(c_ref[...], b_ref[...], (((1,), (1,)), ((), ())), preferred_element_type=F32)
        at = lax.broadcasted_iota(jnp.int32, (length, length), 1)
        kept = jnp.logical_and(
            at <= lax.broadcasted_iota(jnp.int32, (length, length), 0), at + first_ref[0] >= start_ref[...]
        )
        high, low = split2(jnp.where(kept, gram, 0.0))
        g_high[...] = high
        g_low[...] = low
        c_open[...] = jnp.where(start_ref[...] < first_ref[0], c_ref[...].astype(F32), 0.0).astype(BF16)

    x = x_ref[...].astype(F32)
    high, low = split2(spread(weight[...], wide_ref) * x)
    half = lower_ref.shape[0]
    near = jnp.concatenate([upper_ref[:half, :], lower_ref[...]], axis=0)
    entering = near + upper_ref[half : half + 1, :] * far_ref[...]
    e_high, e_low = split2(entering)
    c = c_open[...]
    inner = dot(g_high[...], high) + dot(g_high[...], low) + dot(g_low[...], high) + dot(c, e_high) + dot(c, e_low)
    out_ref[...] = (spread(growth[...], wide_ref) * inner + skip_ref[...] * x).astype(BF16)


def whole(shape):
    return pl.BlockSpec(shape, lambda i: (0,) * len(shape))


def scan_parts(x, step, b_group, c_group, rate, skip, start, first):
    length, width = x.shape
    heads = step.shape[1]
    states = b_group.shape[1]
    chunk = 256
    wide = jnp.repeat(jnp.eye(heads, dtype=BF16), width // heads, axis=1)
    wide = jnp.concatenate([wide] * 3, axis=0)
    rate = rate[None, :]
    start = start[:, None]
    first = jnp.reshape(first, (1,)).astype(jnp.int32)
    smem = pl.BlockSpec(memory_space=pltpu.SMEM)
    columns = lambda rows: pl.BlockSpec((rows, chunk), lambda i: (0, i))
    extra, half = 8, states // 2
    upper, lower = pl.pallas_call(
        state_kernel,
        grid=(width // chunk,),
        in_specs=[
            smem, whole((length, 1)), columns(length), whole((length, heads)), whole((length, states)),
            whole((1, heads)), columns(3 * heads),
        ],
        out_specs=(columns(half + extra), columns(half)),
        out_shape=(
            jax.ShapeDtypeStruct((half + extra, width), F32),
            jax.ShapeDtypeStruct((half, width), F32),
        ),
        scratch_shapes=[pltpu.VMEM((length, heads), F32), pltpu.VMEM((extra, heads), F32)],
        compiler_params=compiler_params(16),
        cost_estimate=pl.CostEstimate(flops=2_000_000_000, bytes_accessed=3_000_000, transcendentals=20_000),
    )(first, start, x, step, b_group, rate, wide)

    def finish(near_upper, near_lower, far):
        return pl.pallas_call(
            scan_kernel,
            grid=(width // chunk,),
            in_specs=[
                smem, whole((length, 1)), columns(length), whole((length, heads)), whole((length, states)),
                whole((length, states)), whole((1, heads)), columns(3 * heads), columns(1),
                columns(half + extra), columns(half), columns(states),
            ],
            out_specs=columns(length),
            out_shape=jax.ShapeDtypeStruct((length, width), BF16),
            scratch_shapes=[
                pltpu.VMEM((length, heads), F32),
                pltpu.VMEM((length, heads), F32),
                pltpu.VMEM((length, length), BF16),
                pltpu.VMEM((length, length), BF16),
                pltpu.VMEM((length, states), BF16),
            ],
            compiler_params=compiler_params(16),
            cost_estimate=pl.CostEstimate(flops=5_000_000_000, bytes_accessed=6_000_000, transcendentals=40_000),
        )(first, start, x, step, b_group, c_group, rate, wide, jnp.repeat(skip, width // heads)[None, :],
            near_upper, near_lower, far)

    return upper, lower, finish


def doc_start(positions, doc_lengths):
    begins = jnp.cumsum(doc_lengths) - doc_lengths
    return jnp.max(jnp.where(begins[None, :] <= positions[:, None], begins[None, :], 0), axis=1).astype(jnp.int32)


def exchange(blocks):
    return lax.all_to_all(blocks, PLANE, split_axis=0, concat_axis=0, tiled=True)


def local(
    queries, keys_in, values_in, ssm_input, step_size, in_proj_b, out_proj_c, decay_rate, skip_gain, doc_lengths
):
    together = lax.optimization_barrier
    block_len = ssm_input.shape[0]
    ctx = lax.axis_index(CTX)
    devices = lax.axis_size(CTX)
    planes = lax.axis_size("z")
    plane_tokens = lax.axis_size(PLANE) * BLOCK
    plane_first = lax.axis_index("z") * plane_tokens
    halo_blocks = MOST_DOC // BLOCK
    to_next = [(i, i + 1) for i in range(planes - 1)]
    k = exchange(turn([keys_in], 60))

    first = ctx * block_len
    start = doc_start(first + jnp.arange(block_len), doc_lengths)
    width = in_proj_b.shape[1] // M_GROUPS
    group = lax.axis_index("y") // (lax.axis_size("y") // M_GROUPS)
    b_group = lax.dynamic_slice_in_dim(in_proj_b, group * width, width, 1)
    c_group = lax.dynamic_slice_in_dim(out_proj_c, group * width, width, 1)
    upper, lower, finish = scan_parts(ssm_input, step_size, b_group, c_group, decay_rate, skip_gain, start, first)
    starts = doc_start(plane_first + jnp.arange(plane_tokens), doc_lengths) - plane_first
    values_in, upper, lower = together((values_in, upper, lower))
    to_next_block = [(i, i + 1) for i in range(devices - 1)]
    near_upper = lax.ppermute(upper, CTX, to_next_block)
    v_blocks, near_upper, starts = together((turn([values_in], 16), near_upper, starts))

    v = exchange(v_blocks)
    halo_k = lax.ppermute(k[-halo_blocks:], "z", to_next)
    own_rows = key_rows(k)
    halo_rows = key_rows(halo_k)
    near_lower = lax.ppermute(lower, CTX, to_next_block)
    q_blocks, own_rows, halo_rows, near_lower = together((turn([queries], 16), own_rows, halo_rows, near_lower))

    q = exchange(q_blocks)
    halo_v = lax.ppermute(v[-halo_blocks:], "z", to_next)
    half = lower.shape[0]
    two = jnp.concatenate([upper[:half], lower], axis=0) + upper[half : half + 1] * jnp.concatenate(
        [near_upper[:half], near_lower], axis=0
    )
    q, halo_v = together((q, halo_v))

    far = lax.ppermute(two, CTX, [(i, i + 2) for i in range(devices - 2)])
    o_blocks, far = together((attend(q, own_rows, v, halo_rows, halo_v, starts), far))

    return turn_back(exchange(o_blocks)), finish(near_upper, near_lower, far)


def solution(mesh):
    ctx, head = mesh.devices.shape
    inner = Mesh(mesh.devices.reshape(4, ctx // 8, 2, head), ("z", "x", "c", "y"))
    everywhere = P(("z", "x", "c", "y"), None)
    return jax.shard_map(
        local,
        mesh=inner,
        in_specs=(
            everywhere, everywhere, everywhere,
            P(CTX, "y"), P(CTX, "y"), P(CTX, None), P(CTX, None), P("y"), P("y"), P(),
        ),
        out_specs=(everywhere, P(CTX, "y")),
        check_vma=False,
    )
```

```python
import functools

import jax
import jax.numpy as jnp
from jax import lax
from jax.experimental import pallas as pl
from jax.experimental.pallas import tpu as pltpu
from jax.sharding import Mesh
from jax.sharding import PartitionSpec as P

ATT_HD = 224
M_HD = 64
M_GROUPS = 2
MOST_DOC = 1536
BLOCK = 128
TILE = 256
GROUP = 2
PLANE = ("x", "c", "y")
CTX = ("z", "x", "c")

F32 = jnp.float32
BF16 = jnp.bfloat16


def compiler_params(mib=48):
    return pltpu.CompilerParams(vmem_limit_bytes=mib * 1024 * 1024)


def split2(value):
    high = value.astype(BF16)
    return high, (value - high.astype(F32)).astype(BF16)


def split3(value):
    high, rest = value.astype(BF16), None
    rest = value - high.astype(F32)
    middle = rest.astype(BF16)
    return high, middle, (rest - middle.astype(F32)).astype(BF16)


def dot(a, b):
    return jnp.dot(a, b, preferred_element_type=F32)


def turn_kernel(count, parts, *refs):
    sources, out, held, turned = refs[:count], refs[count], refs[count + 1 : 2 * count + 1], refs[2 * count + 1]
    in_sems, out_sems = refs[2 * count + 2 :]
    step = turned.shape[0] // parts
    width = step * ATT_HD

    def arriving(i, part):
        columns = pl.ds(part * width, width)
        return pltpu.make_async_copy(sources[i].at[:, columns], held[i].at[:, columns], in_sems.at[i, part])

    def leaving(part):
        rows = pl.ds(part * step, step)
        return pltpu.make_async_copy(turned.at[rows], out.at[rows], out_sems.at[part])

    for part in range(parts):
        for i in range(count):
            arriving(i, part).start()
    for part in range(parts):
        for i in range(count):
            arriving(i, part).wait()
            block = held[i][:, part * width : (part + 1) * width].T
            turned[part * step : (part + 1) * step, i * ATT_HD : (i + 1) * ATT_HD, :] = jnp.reshape(
                block, (step, ATT_HD, BLOCK)
            )
        leaving(part).start()
    for part in range(parts):
        leaving(part).wait()


def turn(arrays, mib):
    count, parts = len(arrays), 4
    width = arrays[0].shape[1]
    heads = width // ATT_HD
    return pl.pallas_call(
        functools.partial(turn_kernel, count, parts),
        in_specs=[pl.BlockSpec(memory_space=pl.ANY)] * count,
        out_specs=pl.BlockSpec(memory_space=pl.ANY),
        out_shape=jax.ShapeDtypeStruct((heads, count * ATT_HD, BLOCK), BF16),
        scratch_shapes=[pltpu.VMEM((BLOCK, width), BF16)] * count
        + [
            pltpu.VMEM((heads, count * ATT_HD, BLOCK), BF16),
            pltpu.SemaphoreType.DMA((count, parts)),
            pltpu.SemaphoreType.DMA((parts,)),
        ],
        compiler_params=compiler_params(mib),
        cost_estimate=pl.CostEstimate(flops=0, bytes_accessed=4 * BLOCK * width * count, transcendentals=0),
    )(*arrays)


def turn_back_kernel(a_ref, out_ref):
    heads = a_ref.shape[0]
    out_ref[...] = jnp.reshape(a_ref[...], (heads * ATT_HD, BLOCK)).T


def turn_back(blocks):
    heads = blocks.shape[0]
    step = 16
    return pl.pallas_call(
        turn_back_kernel,
        grid=(heads // step,),
        in_specs=[pl.BlockSpec((step, ATT_HD, BLOCK), lambda i: (i, 0, 0))],
        out_specs=pl.BlockSpec((BLOCK, step * ATT_HD), lambda i: (0, i)),
        out_shape=jax.ShapeDtypeStruct((BLOCK, heads * ATT_HD), BF16),
        compiler_params=compiler_params(16),
        cost_estimate=pl.CostEstimate(flops=0, bytes_accessed=4 * BLOCK * heads * ATT_HD, transcendentals=0),
    )(blocks)


def key_rows_kernel(k_ref, out_ref):
    for i in range(k_ref.shape[0]):
        out_ref[i * BLOCK : (i + 1) * BLOCK, :] = k_ref[i].T


def key_rows(kv_blocks):
    count = kv_blocks.shape[0]
    step = 4
    return pl.pallas_call(
        key_rows_kernel,
        grid=(count // step,),
        in_specs=[pl.BlockSpec((step, ATT_HD, BLOCK), lambda i: (i, 0, 0))],
        out_specs=pl.BlockSpec((step * BLOCK, ATT_HD), lambda i: (i, 0)),
        out_shape=jax.ShapeDtypeStruct((count * BLOCK, ATT_HD), BF16),
        compiler_params=compiler_params(16),
        cost_estimate=pl.CostEstimate(flops=0, bytes_accessed=4 * count * BLOCK * ATT_HD, transcendentals=0),
    )(kv_blocks)


def attend_kernel(
    most, reach_ref, starts_ref, q_ref, own_k, own_v, halo_k, halo_v, o_ref,
    k_rows, v_cols, q_own, o_own, halo_sems, sems, out_sems,
):
    halo = halo_v.shape[0]
    own = q_ref.shape[0]
    per = TILE // BLOCK
    pairs = own // per // GROUP
    span = GROUP * per

    def arriving(p):
        blocks = pl.ds(span * p, span)
        tokens = span * BLOCK
        return (
            pltpu.make_async_copy(
                own_k.at[pl.ds(pl.multiple_of(p * tokens, tokens), tokens)],
                k_rows.at[pl.ds(pl.multiple_of(halo * BLOCK + p * tokens, tokens), tokens)],
                sems.at[0, p],
            ),
            pltpu.make_async_copy(own_v.at[blocks], v_cols.at[pl.ds(halo + span * p, span)], sems.at[1, p]),
            pltpu.make_async_copy(q_ref.at[blocks], q_own.at[blocks], sems.at[2, p]),
        )

    halo_copies = (
        pltpu.make_async_copy(halo_k, k_rows.at[pl.ds(0, halo * BLOCK)], halo_sems.at[0]),
        pltpu.make_async_copy(halo_v, v_cols.at[pl.ds(0, halo)], halo_sems.at[1]),
    )
    for copy in halo_copies:
        copy.start()

    def begin(p, _):
        for copy in arriving(p):
            copy.start()
        return 0

    lax.fori_loop(0, pairs, begin, 0)
    for copy in halo_copies:
        copy.wait()
    factor = 1.4426950408889634 / ATT_HD**0.5
    down = lax.broadcasted_iota(jnp.int32, (TILE, TILE), 0)
    causal = down <= lax.broadcasted_iota(jnp.int32, (TILE, TILE), 1)

    def out_copy(p):
        blocks = pl.ds(span * p, span)
        return pltpu.make_async_copy(o_own.at[blocks], o_ref.at[blocks], out_sems.at[p])

    def pair(p, _):
        reach = reach_ref[p]
        for copy in arriving(p):
            copy.wait()

        def attend_over(reach):
            first = GROUP * p + halo // per + 1 - reach
            rows = pl.multiple_of(first * TILE, TILE)
            starts = [starts_ref[GROUP * p + part] for part in range(GROUP)]
            counts = [reach + part for part in range(GROUP)]

            def score(part, i):
                s = dot(k_rows[pl.ds(rows + i * TILE, TILE), :], queries)
                kept = down >= starts[part] - (GROUP * p + part - counts[part] + 1 + i) * TILE
                if i == counts[part] - 1:
                    kept = jnp.logical_and(kept, causal)
                return jnp.where(kept, s, -1e30)

            def peak(scores):
                tops = [jnp.max(jnp.reshape(s, (TILE // 8, 8, TILE)), axis=0) for s in scores]
                return jnp.max(functools.reduce(jnp.maximum, tops), axis=0, keepdims=True)

            def values(i):
                return jnp.concatenate([v_cols[first * per + i * per + b] for b in range(per)], axis=1)

            before, top = [], None
            for part in range(GROUP + 1):
                scores, waiting = [], None
                total = jnp.zeros((8, TILE), F32)
                mixed = jnp.zeros((ATT_HD, TILE), F32)
                if part < GROUP:
                    queries = jnp.concatenate([q_own[per * (GROUP * p + part) + b] for b in range(per)], axis=1)
                for i in range(counts[min(part, GROUP - 1)]):
                    if part < GROUP:
                        scores.append(score(part, i))
                    if i < len(before):
                        weights = jnp.exp2((before[i] - top) * factor)
                        total = total + jnp.sum(jnp.reshape(weights, (TILE // 8, 8, TILE)), axis=0)
                        if waiting is not None:
                            mixed = mixed + dot(values(i - 1), waiting)
                        waiting = weights.astype(BF16)
                if part > 0:
                    mixed = mixed + dot(values(len(before) - 1), waiting)
                    out = (mixed * (1.0 / jnp.sum(total, axis=0, keepdims=True))).astype(BF16)
                    for b in range(per):
                        o_own[per * (GROUP * p + part - 1) + b] = out[:, b * BLOCK : (b + 1) * BLOCK]
                if part < GROUP:
                    before, top = scores, peak(scores)

        for count in range(1, most + 1):
            pl.when(reach == count)(functools.partial(attend_over, count))
        out_copy(p).start()
        return 0

    lax.fori_loop(0, pairs, pair, 0)

    def finish(p, _):
        out_copy(p).wait()
        return 0

    lax.fori_loop(0, pairs, finish, 0)


def attend(q_blocks, own_rows, own_v, halo_rows, halo_v, starts):
    own = own_v.shape[0]
    halo = halo_v.shape[0]
    per = TILE // BLOCK
    tiles = own // per
    most = halo // per + 1
    by_tile = jnp.reshape(starts, (tiles, 1, TILE))
    reach = jnp.arange(0, tiles, GROUP, dtype=jnp.int32) - by_tile[::GROUP, 0, 0] // TILE + 1
    vmem = pl.BlockSpec(memory_space=pltpu.VMEM)
    anywhere = pl.BlockSpec(memory_space=pl.ANY)
    return pl.pallas_call(
        functools.partial(attend_kernel, most),
        in_specs=[pl.BlockSpec(memory_space=pltpu.SMEM), vmem] + [anywhere] * 5,
        out_specs=anywhere,
        out_shape=jax.ShapeDtypeStruct((own, ATT_HD, BLOCK), BF16),
        scratch_shapes=[
            pltpu.VMEM(((own + halo) * BLOCK, ATT_HD), BF16),
            pltpu.VMEM((own + halo, ATT_HD, BLOCK), BF16),
            pltpu.VMEM((own, ATT_HD, BLOCK), BF16),
            pltpu.VMEM((own, ATT_HD, BLOCK), BF16),
            pltpu.SemaphoreType.DMA((2,)),
            pltpu.SemaphoreType.DMA((3, tiles // GROUP)),
            pltpu.SemaphoreType.DMA((tiles // GROUP,)),
        ],
        compiler_params=compiler_params(60),
        cost_estimate=pl.CostEstimate(flops=1_000_000, bytes_accessed=1_000_000, transcendentals=0),
    )(reach, by_tile, q_blocks, own_rows, own_v, halo_rows, halo_v)


def cumulative(rate_ref, step_ref):
    length = step_ref.shape[0]
    decay = -rate_ref[...] * step_ref[...]
    order = lax.broadcasted_iota(jnp.int32, (length, length), 0)
    lower = (lax.broadcasted_iota(jnp.int32, (length, length), 1) <= order).astype(F32).astype(BF16)
    a, b, c = split3(decay)
    return dot(lower, a) + dot(lower, b) + dot(lower, c)


def spread(value, wide_ref):
    return dot(jnp.concatenate(split3(value), axis=1), wide_ref[...])


def state_kernel(first_ref, start_ref, x_ref, step_ref, b_ref, rate_ref, wide_ref, upper_ref, lower_ref, weight, passed):
    length = x_ref.shape[0]
    cumul = None

    @pl.when(pl.program_id(0) == 0)
    def _():
        cumul = cumulative(rate_ref, step_ref)
        last = cumul[length - 1 :, :]
        weight[...] = jnp.exp(last - cumul) * step_ref[...]
        linked = jnp.where(start_ref[length - 1 :, :] < first_ref[0], 1.0, 0.0)
        passed[...] = jnp.broadcast_to(jnp.exp(last) * linked, passed.shape)

    last_start = start_ref[length - 1 :, :]
    at = first_ref[0] + lax.broadcasted_iota(jnp.int32, (length, 1), 0)
    same = at >= last_start
    b_same = jnp.where(same, b_ref[...].astype(F32), 0.0).astype(BF16)
    update = spread(weight[...], wide_ref) * x_ref[...].astype(F32)
    high, low = split2(update)
    over = (((0,), (0,)), ((), ()))
    fresh = lax.dot_general(b_same, high, over, preferred_element_type=F32) + lax.dot_general(
        b_same, low, over, preferred_element_type=F32
    )
    half = lower_ref.shape[0]
    upper_ref[:half, :] = fresh[:half]
    upper_ref[half:, :] = spread(passed[...], wide_ref)
    lower_ref[...] = fresh[half:]


def scan_kernel(
    first_ref, start_ref, x_ref, step_ref, b_ref, c_ref, rate_ref, wide_ref, skip_ref,
    upper_ref, lower_ref, far_ref, out_ref, weight, growth, g_high, g_low, c_open,
):
    length = x_ref.shape[0]
    states = b_ref.shape[1]

    @pl.when(pl.program_id(0) == 0)
    def _():
        cumul = cumulative(rate_ref, step_ref)
        growth[...] = jnp.exp(cumul)
        weight[...] = jnp.exp(-cumul) * step_ref[...]
        gram = lax.dot_general(c_ref[...], b_ref[...], (((1,), (1,)), ((), ())), preferred_element_type=F32)
        at = lax.broadcasted_iota(jnp.int32, (length, length), 1)
        kept = jnp.logical_and(
            at <= lax.broadcasted_iota(jnp.int32, (length, length), 0), at + first_ref[0] >= start_ref[...]
        )
        high, low = split2(jnp.where(kept, gram, 0.0))
        g_high[...] = high
        g_low[...] = low
        c_open[...] = jnp.where(start_ref[...] < first_ref[0], c_ref[...].astype(F32), 0.0).astype(BF16)

    x = x_ref[...].astype(F32)
    high, low = split2(spread(weight[...], wide_ref) * x)
    half = lower_ref.shape[0]
    near = jnp.concatenate([upper_ref[:half, :], lower_ref[...]], axis=0)
    entering = near + upper_ref[half : half + 1, :] * far_ref[...]
    e_high, e_low = split2(entering)
    c = c_open[...]
    inner = dot(g_high[...], high) + dot(g_high[...], low) + dot(g_low[...], high) + dot(c, e_high) + dot(c, e_low)
    out_ref[...] = (spread(growth[...], wide_ref) * inner + skip_ref[...] * x).astype(BF16)


def whole(shape):
    return pl.BlockSpec(shape, lambda i: (0,) * len(shape))


def scan_parts(x, step, b_group, c_group, rate, skip, start, first):
    length, width = x.shape
    heads = step.shape[1]
    states = b_group.shape[1]
    chunk = 256
    wide = jnp.repeat(jnp.eye(heads, dtype=BF16), width // heads, axis=1)
    wide = jnp.concatenate([wide] * 3, axis=0)
    rate = rate[None, :]
    start = start[:, None]
    first = jnp.reshape(first, (1,)).astype(jnp.int32)
    smem = pl.BlockSpec(memory_space=pltpu.SMEM)
    columns = lambda rows: pl.BlockSpec((rows, chunk), lambda i: (0, i))
    extra, half = 8, states // 2
    upper, lower = pl.pallas_call(
        state_kernel,
        grid=(width // chunk,),
        in_specs=[
            smem, whole((length, 1)), columns(length), whole((length, heads)), whole((length, states)),
            whole((1, heads)), columns(3 * heads),
        ],
        out_specs=(columns(half + extra), columns(half)),
        out_shape=(
            jax.ShapeDtypeStruct((half + extra, width), F32),
            jax.ShapeDtypeStruct((half, width), F32),
        ),
        scratch_shapes=[pltpu.VMEM((length, heads), F32), pltpu.VMEM((extra, heads), F32)],
        compiler_params=compiler_params(16),
        cost_estimate=pl.CostEstimate(flops=2_000_000_000, bytes_accessed=3_000_000, transcendentals=20_000),
    )(first, start, x, step, b_group, rate, wide)

    def finish(near_upper, near_lower, far):
        return pl.pallas_call(
            scan_kernel,
            grid=(width // chunk,),
            in_specs=[
                smem, whole((length, 1)), columns(length), whole((length, heads)), whole((length, states)),
                whole((length, states)), whole((1, heads)), columns(3 * heads), columns(1),
                columns(half + extra), columns(half), columns(states),
            ],
            out_specs=columns(length),
            out_shape=jax.ShapeDtypeStruct((length, width), BF16),
            scratch_shapes=[
                pltpu.VMEM((length, heads), F32),
                pltpu.VMEM((length, heads), F32),
                pltpu.VMEM((length, length), BF16),
                pltpu.VMEM((length, length), BF16),
                pltpu.VMEM((length, states), BF16),
            ],
            compiler_params=compiler_params(16),
            cost_estimate=pl.CostEstimate(flops=5_000_000_000, bytes_accessed=6_000_000, transcendentals=40_000),
        )(first, start, x, step, b_group, c_group, rate, wide, jnp.repeat(skip, width // heads)[None, :],
            near_upper, near_lower, far)

    return upper, lower, finish


def doc_start(positions, doc_lengths):
    begins = jnp.cumsum(doc_lengths) - doc_lengths
    return jnp.max(jnp.where(begins[None, :] <= positions[:, None], begins[None, :], 0), axis=1).astype(jnp.int32)


def exchange(blocks):
    return lax.all_to_all(blocks, PLANE, split_axis=0, concat_axis=0, tiled=True)


def local(
    queries, keys_in, values_in, ssm_input, step_size, in_proj_b, out_proj_c, decay_rate, skip_gain, doc_lengths
):
    together = lax.optimization_barrier
    block_len = ssm_input.shape[0]
    ctx = lax.axis_index(CTX)
    devices = lax.axis_size(CTX)
    planes = lax.axis_size("z")
    plane_tokens = lax.axis_size(PLANE) * BLOCK
    plane_first = lax.axis_index("z") * plane_tokens
    halo_blocks = MOST_DOC // BLOCK
    to_next = [(i, i + 1) for i in range(planes - 1)]
    k = exchange(turn([keys_in], 60))

    first = ctx * block_len
    start = doc_start(first + jnp.arange(block_len), doc_lengths)
    width = in_proj_b.shape[1] // M_GROUPS
    group = lax.axis_index("y") // (lax.axis_size("y") // M_GROUPS)
    b_group = lax.dynamic_slice_in_dim(in_proj_b, group * width, width, 1)
    c_group = lax.dynamic_slice_in_dim(out_proj_c, group * width, width, 1)
    upper, lower, finish = scan_parts(ssm_input, step_size, b_group, c_group, decay_rate, skip_gain, start, first)
    starts = doc_start(plane_first + jnp.arange(plane_tokens), doc_lengths) - plane_first
    values_in, upper, lower = together((values_in, upper, lower))
    to_next_block = [(i, i + 1) for i in range(devices - 1)]
    near_upper = lax.ppermute(upper, CTX, to_next_block)
    v_blocks, near_upper, starts = together((turn([values_in], 16), near_upper, starts))

    v = exchange(v_blocks)
    halo_k = lax.ppermute(k[-halo_blocks:], "z", to_next)
    own_rows = key_rows(k)
    near_lower = lax.ppermute(lower, CTX, to_next_block)
    queries, near_lower = together((queries, near_lower))
    q_blocks, own_rows, halo_k = together((turn([queries], 16), own_rows, halo_k))
    halo_rows = key_rows(halo_k)

    q = exchange(q_blocks)
    halo_v = lax.ppermute(v[-halo_blocks:], "z", to_next)
    half = lower.shape[0]
    two = jnp.concatenate([upper[:half], lower], axis=0) + upper[half : half + 1] * jnp.concatenate(
        [near_upper[:half], near_lower], axis=0
    )
    q, halo_v = together((q, halo_v))

    far = lax.ppermute(two, CTX, [(i, i + 2) for i in range(devices - 2)])
    o_blocks, far = together((attend(q, own_rows, v, halo_rows, halo_v, starts), far))

    return turn_back(exchange(o_blocks)), finish(near_upper, near_lower, far)


def solution(mesh):
    ctx, head = mesh.devices.shape
    inner = Mesh(mesh.devices.reshape(4, ctx // 8, 2, head), ("z", "x", "c", "y"))
    everywhere = P(("z", "x", "c", "y"), None)
    return jax.shard_map(
        local,
        mesh=inner,
        in_specs=(
            everywhere, everywhere, everywhere,
            P(CTX, "y"), P(CTX, "y"), P(CTX, None), P(CTX, None), P("y"), P("y"), P(),
        ),
        out_specs=(everywhere, P(CTX, "y")),
        check_vma=False,
    )
```

```python
import functools

import jax
import jax.numpy as jnp
from jax import lax
from jax.experimental import pallas as pl
from jax.experimental.pallas import tpu as pltpu
from jax.sharding import Mesh
from jax.sharding import PartitionSpec as P

ATT_HD = 224
M_HD = 64
M_GROUPS = 2
MOST_DOC = 1536
BLOCK = 128
TILE = 256
GROUP = 2
PLANE = ("x", "c", "y")
CTX = ("z", "x", "c")

F32 = jnp.float32
BF16 = jnp.bfloat16


def compiler_params(mib=48):
    return pltpu.CompilerParams(vmem_limit_bytes=mib * 1024 * 1024)


def split2(value):
    high = value.astype(BF16)
    return high, (value - high.astype(F32)).astype(BF16)


def split3(value):
    high, rest = value.astype(BF16), None
    rest = value - high.astype(F32)
    middle = rest.astype(BF16)
    return high, middle, (rest - middle.astype(F32)).astype(BF16)


def dot(a, b):
    return jnp.dot(a, b, preferred_element_type=F32)


def turn_kernel(count, parts, *refs):
    sources, out, held, turned = refs[:count], refs[count], refs[count + 1 : 2 * count + 1], refs[2 * count + 1]
    in_sems, out_sems = refs[2 * count + 2 :]
    step = turned.shape[0] // parts
    width = step * ATT_HD

    def arriving(i, part):
        columns = pl.ds(part * width, width)
        return pltpu.make_async_copy(sources[i].at[:, columns], held[i].at[:, columns], in_sems.at[i, part])

    def leaving(part):
        rows = pl.ds(part * step, step)
        return pltpu.make_async_copy(turned.at[rows], out.at[rows], out_sems.at[part])

    for part in range(parts):
        for i in range(count):
            arriving(i, part).start()
    for part in range(parts):
        for i in range(count):
            arriving(i, part).wait()
            block = held[i][:, part * width : (part + 1) * width].T
            turned[part * step : (part + 1) * step, i * ATT_HD : (i + 1) * ATT_HD, :] = jnp.reshape(
                block, (step, ATT_HD, BLOCK)
            )
        leaving(part).start()
    for part in range(parts):
        leaving(part).wait()


def turn(arrays, mib):
    count, parts = len(arrays), 4
    width = arrays[0].shape[1]
    heads = width // ATT_HD
    return pl.pallas_call(
        functools.partial(turn_kernel, count, parts),
        in_specs=[pl.BlockSpec(memory_space=pl.ANY)] * count,
        out_specs=pl.BlockSpec(memory_space=pl.ANY),
        out_shape=jax.ShapeDtypeStruct((heads, count * ATT_HD, BLOCK), BF16),
        scratch_shapes=[pltpu.VMEM((BLOCK, width), BF16)] * count
        + [
            pltpu.VMEM((heads, count * ATT_HD, BLOCK), BF16),
            pltpu.SemaphoreType.DMA((count, parts)),
            pltpu.SemaphoreType.DMA((parts,)),
        ],
        compiler_params=compiler_params(mib),
        cost_estimate=pl.CostEstimate(flops=0, bytes_accessed=4 * BLOCK * width * count, transcendentals=0),
    )(*arrays)


def turn_back_kernel(a_ref, out_ref):
    heads = a_ref.shape[0]
    out_ref[...] = jnp.reshape(a_ref[...], (heads * ATT_HD, BLOCK)).T


def turn_back(blocks):
    heads = blocks.shape[0]
    step = 16
    return pl.pallas_call(
        turn_back_kernel,
        grid=(heads // step,),
        in_specs=[pl.BlockSpec((step, ATT_HD, BLOCK), lambda i: (i, 0, 0))],
        out_specs=pl.BlockSpec((BLOCK, step * ATT_HD), lambda i: (0, i)),
        out_shape=jax.ShapeDtypeStruct((BLOCK, heads * ATT_HD), BF16),
        compiler_params=compiler_params(16),
        cost_estimate=pl.CostEstimate(flops=0, bytes_accessed=4 * BLOCK * heads * ATT_HD, transcendentals=0),
    )(blocks)


def key_rows_kernel(k_ref, out_ref):
    for i in range(k_ref.shape[0]):
        out_ref[i * BLOCK : (i + 1) * BLOCK, :] = k_ref[i].T


def key_rows(kv_blocks):
    count = kv_blocks.shape[0]
    step = 4
    return pl.pallas_call(
        key_rows_kernel,
        grid=(count // step,),
        in_specs=[pl.BlockSpec((step, ATT_HD, BLOCK), lambda i: (i, 0, 0))],
        out_specs=pl.BlockSpec((step * BLOCK, ATT_HD), lambda i: (i, 0)),
        out_shape=jax.ShapeDtypeStruct((count * BLOCK, ATT_HD), BF16),
        compiler_params=compiler_params(16),
        cost_estimate=pl.CostEstimate(flops=0, bytes_accessed=4 * count * BLOCK * ATT_HD, transcendentals=0),
    )(kv_blocks)


def attend_kernel(
    most, reach_ref, starts_ref, q_ref, own_k, own_v, halo_k, halo_v, o_ref,
    k_rows, v_cols, q_own, o_own, halo_sems, sems, out_sems,
):
    halo = halo_v.shape[0]
    own = q_ref.shape[0]
    per = TILE // BLOCK
    pairs = own // per // GROUP
    span = GROUP * per

    def arriving(p):
        blocks = pl.ds(span * p, span)
        tokens = span * BLOCK
        return (
            pltpu.make_async_copy(
                own_k.at[pl.ds(pl.multiple_of(p * tokens, tokens), tokens)],
                k_rows.at[pl.ds(pl.multiple_of(halo * BLOCK + p * tokens, tokens), tokens)],
                sems.at[0, p],
            ),
            pltpu.make_async_copy(own_v.at[blocks], v_cols.at[pl.ds(halo + span * p, span)], sems.at[1, p]),
            pltpu.make_async_copy(q_ref.at[blocks], q_own.at[blocks], sems.at[2, p]),
        )

    halo_copies = (
        pltpu.make_async_copy(halo_k, k_rows.at[pl.ds(0, halo * BLOCK)], halo_sems.at[0]),
        pltpu.make_async_copy(halo_v, v_cols.at[pl.ds(0, halo)], halo_sems.at[1]),
    )
    for copy in halo_copies:
        copy.start()

    def begin(p, _):
        for copy in arriving(p):
            copy.start()
        return 0

    lax.fori_loop(0, pairs, begin, 0)
    for copy in halo_copies:
        copy.wait()
    factor = 1.4426950408889634 / ATT_HD**0.5
    down = lax.broadcasted_iota(jnp.int32, (TILE, TILE), 0)
    causal = down <= lax.broadcasted_iota(jnp.int32, (TILE, TILE), 1)

    def out_copy(p):
        blocks = pl.ds(span * p, span)
        return pltpu.make_async_copy(o_own.at[blocks], o_ref.at[blocks], out_sems.at[p])

    def pair(p, _):
        reach = reach_ref[p]
        for copy in arriving(p):
            copy.wait()

        def attend_over(reach):
            first = GROUP * p + halo // per + 1 - reach
            rows = pl.multiple_of(first * TILE, TILE)
            starts = [starts_ref[GROUP * p + part] for part in range(GROUP)]
            counts = [reach + part for part in range(GROUP)]

            def score(part, i):
                s = dot(k_rows[pl.ds(rows + i * TILE, TILE), :], queries)
                kept = down >= starts[part] - (GROUP * p + part - counts[part] + 1 + i) * TILE
                if i == counts[part] - 1:
                    kept = jnp.logical_and(kept, causal)
                return jnp.where(kept, s, -1e30)

            def peak(scores):
                tops = [jnp.max(jnp.reshape(s, (TILE // 8, 8, TILE)), axis=0) for s in scores]
                return jnp.max(functools.reduce(jnp.maximum, tops), axis=0, keepdims=True)

            def values(i):
                return jnp.concatenate([v_cols[first * per + i * per + b] for b in range(per)], axis=1)

            before, top = [], None
            for part in range(GROUP + 1):
                scores, waiting = [], None
                total = jnp.zeros((8, TILE), F32)
                mixed = jnp.zeros((ATT_HD, TILE), F32)
                if part < GROUP:
                    queries = jnp.concatenate([q_own[per * (GROUP * p + part) + b] for b in range(per)], axis=1)
                for i in range(counts[min(part, GROUP - 1)]):
                    if part < GROUP:
                        scores.append(score(part, i))
                    if i < len(before):
                        weights = jnp.exp2((before[i] - top) * factor)
                        total = total + jnp.sum(jnp.reshape(weights, (TILE // 8, 8, TILE)), axis=0)
                        if waiting is not None:
                            mixed = mixed + dot(values(i - 1), waiting)
                        waiting = weights.astype(BF16)
                if part > 0:
                    mixed = mixed + dot(values(len(before) - 1), waiting)
                    out = (mixed * (1.0 / jnp.sum(total, axis=0, keepdims=True))).astype(BF16)
                    for b in range(per):
                        o_own[per * (GROUP * p + part - 1) + b] = out[:, b * BLOCK : (b + 1) * BLOCK]
                if part < GROUP:
                    before, top = scores, peak(scores)

        for count in range(1, most + 1):
            pl.when(reach == count)(functools.partial(attend_over, count))
        out_copy(p).start()
        return 0

    lax.fori_loop(0, pairs, pair, 0)

    def finish(p, _):
        out_copy(p).wait()
        return 0

    lax.fori_loop(0, pairs, finish, 0)


def attend(q_blocks, own_rows, own_v, halo_rows, halo_v, starts):
    own = own_v.shape[0]
    halo = halo_v.shape[0]
    per = TILE // BLOCK
    tiles = own // per
    most = halo // per + 1
    by_tile = jnp.reshape(starts, (tiles, 1, TILE))
    reach = jnp.arange(0, tiles, GROUP, dtype=jnp.int32) - by_tile[::GROUP, 0, 0] // TILE + 1
    vmem = pl.BlockSpec(memory_space=pltpu.VMEM)
    anywhere = pl.BlockSpec(memory_space=pl.ANY)
    return pl.pallas_call(
        functools.partial(attend_kernel, most),
        in_specs=[pl.BlockSpec(memory_space=pltpu.SMEM), vmem] + [anywhere] * 5,
        out_specs=anywhere,
        out_shape=jax.ShapeDtypeStruct((own, ATT_HD, BLOCK), BF16),
        scratch_shapes=[
            pltpu.VMEM(((own + halo) * BLOCK, ATT_HD), BF16),
            pltpu.VMEM((own + halo, ATT_HD, BLOCK), BF16),
            pltpu.VMEM((own, ATT_HD, BLOCK), BF16),
            pltpu.VMEM((own, ATT_HD, BLOCK), BF16),
            pltpu.SemaphoreType.DMA((2,)),
            pltpu.SemaphoreType.DMA((3, tiles // GROUP)),
            pltpu.SemaphoreType.DMA((tiles // GROUP,)),
        ],
        compiler_params=compiler_params(60),
        cost_estimate=pl.CostEstimate(flops=1_000_000, bytes_accessed=1_000_000, transcendentals=0),
    )(reach, by_tile, q_blocks, own_rows, own_v, halo_rows, halo_v)


def cumulative(rate_ref, step_ref):
    length = step_ref.shape[0]
    decay = -rate_ref[...] * step_ref[...]
    order = lax.broadcasted_iota(jnp.int32, (length, length), 0)
    lower = (lax.broadcasted_iota(jnp.int32, (length, length), 1) <= order).astype(F32).astype(BF16)
    a, b, c = split3(decay)
    return dot(lower, a) + dot(lower, b) + dot(lower, c)


def spread(value, wide_ref):
    return dot(jnp.concatenate(split3(value), axis=1), wide_ref[...])


def state_kernel(first_ref, start_ref, x_ref, step_ref, b_ref, rate_ref, wide_ref, upper_ref, lower_ref, weight, passed):
    length = x_ref.shape[0]
    cumul = None

    @pl.when(pl.program_id(0) == 0)
    def _():
        cumul = cumulative(rate_ref, step_ref)
        last = cumul[length - 1 :, :]
        weight[...] = jnp.exp(last - cumul) * step_ref[...]
        linked = jnp.where(start_ref[length - 1 :, :] < first_ref[0], 1.0, 0.0)
        passed[...] = jnp.broadcast_to(jnp.exp(last) * linked, passed.shape)

    last_start = start_ref[length - 1 :, :]
    at = first_ref[0] + lax.broadcasted_iota(jnp.int32, (length, 1), 0)
    same = at >= last_start
    b_same = jnp.where(same, b_ref[...].astype(F32), 0.0).astype(BF16)
    update = spread(weight[...], wide_ref) * x_ref[...].astype(F32)
    high, low = split2(update)
    over = (((0,), (0,)), ((), ()))
    fresh = lax.dot_general(b_same, high, over, preferred_element_type=F32) + lax.dot_general(
        b_same, low, over, preferred_element_type=F32
    )
    half = fresh.shape[0] - lower_ref.shape[0]
    upper_ref[:half, :] = fresh[:half]
    upper_ref[half:, :] = spread(passed[...], wide_ref)
    lower_ref[...] = fresh[half:]


def scan_kernel(
    first_ref, start_ref, x_ref, step_ref, b_ref, c_ref, rate_ref, wide_ref, skip_ref,
    upper_ref, lower_ref, far_ref, out_ref, weight, growth, g_high, g_low, c_open,
):
    length = x_ref.shape[0]
    states = b_ref.shape[1]

    @pl.when(pl.program_id(0) == 0)
    def _():
        cumul = cumulative(rate_ref, step_ref)
        growth[...] = jnp.exp(cumul)
        weight[...] = jnp.exp(-cumul) * step_ref[...]
        gram = lax.dot_general(c_ref[...], b_ref[...], (((1,), (1,)), ((), ())), preferred_element_type=F32)
        at = lax.broadcasted_iota(jnp.int32, (length, length), 1)
        kept = jnp.logical_and(
            at <= lax.broadcasted_iota(jnp.int32, (length, length), 0), at + first_ref[0] >= start_ref[...]
        )
        high, low = split2(jnp.where(kept, gram, 0.0))
        g_high[...] = high
        g_low[...] = low
        c_open[...] = jnp.where(start_ref[...] < first_ref[0], c_ref[...].astype(F32), 0.0).astype(BF16)

    x = x_ref[...].astype(F32)
    high, low = split2(spread(weight[...], wide_ref) * x)
    half = states - lower_ref.shape[0]
    near = jnp.concatenate([upper_ref[:half, :], lower_ref[...]], axis=0)
    entering = near + upper_ref[half : half + 1, :] * far_ref[...]
    e_high, e_low = split2(entering)
    c = c_open[...]
    inner = dot(g_high[...], high) + dot(g_high[...], low) + dot(g_low[...], high) + dot(c, e_high) + dot(c, e_low)
    out_ref[...] = (spread(growth[...], wide_ref) * inner + skip_ref[...] * x).astype(BF16)


def whole(shape):
    return pl.BlockSpec(shape, lambda i: (0,) * len(shape))


def scan_parts(x, step, b_group, c_group, rate, skip, start, first):
    length, width = x.shape
    heads = step.shape[1]
    states = b_group.shape[1]
    chunk = 256
    wide = jnp.repeat(jnp.eye(heads, dtype=BF16), width // heads, axis=1)
    wide = jnp.concatenate([wide] * 3, axis=0)
    rate = rate[None, :]
    start = start[:, None]
    first = jnp.reshape(first, (1,)).astype(jnp.int32)
    smem = pl.BlockSpec(memory_space=pltpu.SMEM)
    columns = lambda rows: pl.BlockSpec((rows, chunk), lambda i: (0, i))
    extra, half = 8, states * 3 // 4
    upper, lower = pl.pallas_call(
        state_kernel,
        grid=(width // chunk,),
        in_specs=[
            smem, whole((length, 1)), columns(length), whole((length, heads)), whole((length, states)),
            whole((1, heads)), columns(3 * heads),
        ],
        out_specs=(columns(half + extra), columns(states - half)),
        out_shape=(
            jax.ShapeDtypeStruct((half + extra, width), F32),
            jax.ShapeDtypeStruct((states - half, width), F32),
        ),
        scratch_shapes=[pltpu.VMEM((length, heads), F32), pltpu.VMEM((extra, heads), F32)],
        compiler_params=compiler_params(16),
        cost_estimate=pl.CostEstimate(flops=2_000_000_000, bytes_accessed=3_000_000, transcendentals=20_000),
    )(first, start, x, step, b_group, rate, wide)

    def finish(near_upper, near_lower, far):
        return pl.pallas_call(
            scan_kernel,
            grid=(width // chunk,),
            in_specs=[
                smem, whole((length, 1)), columns(length), whole((length, heads)), whole((length, states)),
                whole((length, states)), whole((1, heads)), columns(3 * heads), columns(1),
                columns(half + extra), columns(states - half), columns(states),
            ],
            out_specs=columns(length),
            out_shape=jax.ShapeDtypeStruct((length, width), BF16),
            scratch_shapes=[
                pltpu.VMEM((length, heads), F32),
                pltpu.VMEM((length, heads), F32),
                pltpu.VMEM((length, length), BF16),
                pltpu.VMEM((length, length), BF16),
                pltpu.VMEM((length, states), BF16),
            ],
            compiler_params=compiler_params(16),
            cost_estimate=pl.CostEstimate(flops=5_000_000_000, bytes_accessed=6_000_000, transcendentals=40_000),
        )(first, start, x, step, b_group, c_group, rate, wide, jnp.repeat(skip, width // heads)[None, :],
            near_upper, near_lower, far)

    return upper, lower, finish


def doc_start(positions, doc_lengths):
    begins = jnp.cumsum(doc_lengths) - doc_lengths
    return jnp.max(jnp.where(begins[None, :] <= positions[:, None], begins[None, :], 0), axis=1).astype(jnp.int32)


def exchange(blocks):
    return lax.all_to_all(blocks, PLANE, split_axis=0, concat_axis=0, tiled=True)


def local(
    queries, keys_in, values_in, ssm_input, step_size, in_proj_b, out_proj_c, decay_rate, skip_gain, doc_lengths
):
    together = lax.optimization_barrier
    block_len = ssm_input.shape[0]
    ctx = lax.axis_index(CTX)
    devices = lax.axis_size(CTX)
    planes = lax.axis_size("z")
    plane_tokens = lax.axis_size(PLANE) * BLOCK
    plane_first = lax.axis_index("z") * plane_tokens
    halo_blocks = MOST_DOC // BLOCK
    to_next = [(i, i + 1) for i in range(planes - 1)]
    k = exchange(turn([keys_in], 60))

    first = ctx * block_len
    start = doc_start(first + jnp.arange(block_len), doc_lengths)
    width = in_proj_b.shape[1] // M_GROUPS
    group = lax.axis_index("y") // (lax.axis_size("y") // M_GROUPS)
    b_group = lax.dynamic_slice_in_dim(in_proj_b, group * width, width, 1)
    c_group = lax.dynamic_slice_in_dim(out_proj_c, group * width, width, 1)
    upper, lower, finish = scan_parts(ssm_input, step_size, b_group, c_group, decay_rate, skip_gain, start, first)
    starts = doc_start(plane_first + jnp.arange(plane_tokens), doc_lengths) - plane_first
    values_in, upper, lower = together((values_in, upper, lower))
    to_next_block = [(i, i + 1) for i in range(devices - 1)]
    near_upper = lax.ppermute(upper, CTX, to_next_block)
    v_blocks, near_upper, starts = together((turn([values_in], 16), near_upper, starts))

    v = exchange(v_blocks)
    halo_k = lax.ppermute(k[-halo_blocks:], "z", to_next)
    own_rows = key_rows(k)
    halo_rows = key_rows(halo_k)
    near_lower = lax.ppermute(lower, CTX, to_next_block)
    q_blocks, own_rows, halo_rows, near_lower = together((turn([queries], 16), own_rows, halo_rows, near_lower))

    q = exchange(q_blocks)
    halo_v = lax.ppermute(v[-halo_blocks:], "z", to_next)
    half = width - lower.shape[0]
    two = jnp.concatenate([upper[:half], lower], axis=0) + upper[half : half + 1] * jnp.concatenate(
        [near_upper[:half], near_lower], axis=0
    )
    q, halo_v = together((q, halo_v))

    far = lax.ppermute(two, CTX, [(i, i + 2) for i in range(devices - 2)])
    o_blocks, far = together((attend(q, own_rows, v, halo_rows, halo_v, starts), far))

    return turn_back(exchange(o_blocks)), finish(near_upper, near_lower, far)


def solution(mesh):
    ctx, head = mesh.devices.shape
    inner = Mesh(mesh.devices.reshape(4, ctx // 8, 2, head), ("z", "x", "c", "y"))
    everywhere = P(("z", "x", "c", "y"), None)
    return jax.shard_map(
        local,
        mesh=inner,
        in_specs=(
            everywhere, everywhere, everywhere,
            P(CTX, "y"), P(CTX, "y"), P(CTX, None), P(CTX, None), P("y"), P("y"), P(),
        ),
        out_specs=(everywhere, P(CTX, "y")),
        check_vma=False,
    )
```
